128 devices in a mesh: role: 4 (over y), dom: 32 (over x, z, core).
Axes of the slice: x: 4, y: 4, z: 4, core: 2. Of those that a mesh axis runs over, the one named last changes fastest.
Arguments:
- tire_pos: float32 [3, 1572864], P(None, ('role', 'dom')), may hold values from -6 to 6
- tire_vel: float32 [3, 1572864], P(None, ('role', 'dom')), may hold values from -3 to 3
- part_pos: float32 [3, 1048576], P(None, ('role', 'dom')), may hold values from -6 to 6
- part_vel: float32 [3, 1048576], P(None, ('role', 'dom')), may hold values from -3 to 3
- contact_owner: int32 [12288, 2], P(('role', 'dom')), may hold values from 0 to 127, all different within a row; in each aligned block of 96 rows (0 to 95, 96 to 191, ...) at most 2 rows name the same one
- contact_tile: int32 [12288, 2], P(('role', 'dom')), may hold values from 0 to 63
- halo_tiles: int32 [512], P(('role', 'dom')), may hold values from 0 to 63
- block_inverse: float32 [12288, 128, 128], P(('role', 'dom')), may hold values from -1 to 1, as said below
- pattern: int32 [12288, 3], P(('role', 'dom')), may hold values from 0 to 95
- coupling: float32 [12288, 3], P(('role', 'dom')), may hold values from 0.05 to 0.2
Outputs:
- tire_pos_out: float32 [3, 1572864], P(None, ('role', 'dom'))
- tire_vel_out: float32 [3, 1572864], P(None, ('role', 'dom'))
- part_pos_out: float32 [3, 1048576], P(None, ('role', 'dom'))
- part_vel_out: float32 [3, 1048576], P(None, ('role', 'dom'))
The draws below stay inside these ranges and needn't reach their ends.
Inputs may be any that keep to these rules, and one draw needn't show every extreme that they name: `contact_owner`: among the 96 rows of one device, no owner is named by more than 2 rows, a bound that some block reaches; each row names 2 different owners. `block_inverse`: each block has its diagonal near 0.6.
All inputs are finite; a program needn't handle non-finite values.
Results may differ from the reference program's by a relative error of at most 0.0001.
Values sent between devices are 32-bit elements; how exact they have to be, the bound alone decides.
A program may use at most 64 MiB of HBM per device.

```python
import math
import jax
import jax.numpy as jnp
import numpy as np
from jax import lax

BLK = 128
NB_DEV = 96
TILES_DEV = 64
TOPC = 2
CAP = 2
HB = 4
NNZB = 3
STEPS = 2
SWEEPS = 3
BLOCKS = 12288
NODES = 1572864
PARTICLES = 1048576
N_ROLE = 4
N_DOM = 32


def draw_block_inverse(key, part):
    key = jax.random.fold_in(key, 7)
    shape = (BLOCKS, BLK, BLK)
    identity = (lax.broadcasted_iota(jnp.int32, shape, 1) == lax.broadcasted_iota(jnp.int32, shape, 2)).astype(jnp.float32)
    noise = jax.random.uniform(key, shape, jnp.float32, -0.85, 0.85) / math.sqrt(BLK)
    return 0.6 * identity + noise


def set_ends(values, own_key, low, top_value):
    shape = values.shape
    place = [jax.random.randint(jax.random.fold_in(own_key, axis), (), 0, shape[axis]) for axis in range(len(shape))]
    values = values.at[tuple(place)].set(low)
    longest = shape.index(max(shape))
    place[longest] = (place[longest] + 1) % shape[longest]
    return values.at[tuple(place)].set(top_value)


def block_levels(key, shape, pieces, least, top_value):
    factor_of, own = 1.0, jax.random.fold_in(key, 6)
    for dim, shards_of in pieces:
        steps = jnp.exp(jax.random.uniform(jax.random.fold_in(own, dim), (shards_of,), jnp.float32, least / len(pieces), top_value / len(pieces)))
        factor_of = factor_of * jnp.repeat(steps, shape[dim] // shards_of).reshape([-1 if axis == dim else 1 for axis in range(len(shape))])
    return factor_of


def shared_out(rng, own, number, rows, number_of, top, bound, slope):
    order = jax.random.permutation(rng, number_of)
    packed, ordinary = shares(number_of, rows * top, bound, slope, True), shares(number_of, rows * top, bound, slope, False)
    places = jnp.arange(number_of)

    def named(tallies, turn):
        used = int((tallies > 0).sum())
        fixed = max(1, used // 4)
        shifted = fixed + (places - fixed + turn * (used - fixed)) % max(1, number_of - fixed)
        return jnp.zeros((number_of,), jnp.int32).at[order[jnp.where(places < fixed, places, shifted)]].set(jnp.asarray(tallies, jnp.int32))

    tallies = jnp.where(number % 4 == 0, named(packed, number // 4), named(ordinary, number - number // 4 - 1))
    mixed = jax.random.permutation(jax.random.fold_in(own, 3), number_of)
    donor, receiver = mixed[0:number_of // 2 * 2:2], mixed[1:number_of // 2 * 2:2]
    margin = jnp.minimum(tallies[donor] - 1, bound - tallies[receiver]) // 2
    margin = jnp.where((donor == order[0]) | (receiver == order[0]) | (tallies[receiver] == 0), 0, jnp.maximum(margin, 0))
    shifted = jax.random.randint(jax.random.fold_in(own, 4), (number_of // 2,), 0, 1 << 20) % (margin + 1)
    tallies = tallies.at[donor].add(-shifted).at[receiver].add(shifted)
    items = jnp.searchsorted(jnp.cumsum(tallies), jnp.arange(rows * top), side="right").astype(jnp.int32)
    table = items.reshape(top, rows).T
    table = table[jax.random.permutation(jax.random.fold_in(own, 1), rows)]
    turn = jax.random.randint(jax.random.fold_in(own, 2), (rows, 1), 0, top)
    return jnp.take_along_axis(table, (jnp.arange(top)[None, :] + turn) % top, axis=1)


def shares(number_of, total, most, slope, full):
    portions = [(1 << 20) // math.isqrt(standing ** slope) + 1 for standing in range(1, number_of + 1)]
    largest = most if full else min(most, max(-(-total // number_of), total * portions[0] // sum(portions)))
    least = 1 if total - largest >= number_of - 1 else 0
    holding, spare = [largest] + [least] * (number_of - 1), total - largest - least * (number_of - 1)
    while spare > 0:
        free = [i for i in range(1, number_of) if holding[i] < largest] or [i for i in range(1, number_of) if holding[i] < most]
        pool, remaining = sum([portions[i] for i in free]), spare
        for i in free:
            more = min(most - holding[i], max(1, remaining * portions[i] // pool), spare)
            holding[i] = holding[i] + more
            spare = spare - more
    return np.array(holding)


def normal_values(own_key, dims, width, limit, shards=(), held_as=jnp.bfloat16):
    array = jax.random.normal(own_key, dims, jnp.float32) * width
    if len(shards) > 0:
        array = block_levels(own_key, dims, shards, -0.22, 0.18) * array
    return jnp.clip(array, min=-limit, max=limit).astype(held_as)


def setup_inputs(seed: int = 0) -> dict:
    splits = jax.random.split(jax.random.key(seed), 11)
    tire_pos = normal_values(splits[0], (3, NODES), 1.0, 6.0, ((1, 128),), jnp.float32)
    tire_vel = normal_values(splits[1], (3, NODES), 0.5, 3.0, ((1, 128),), jnp.float32)
    part_pos = normal_values(splits[2], (3, PARTICLES), 1.0, 6.0, ((1, 128),), jnp.float32)
    part_vel = normal_values(splits[3], (3, PARTICLES), 0.5, 3.0, ((1, 128),), jnp.float32)
    contact_owner_keys = jax.random.split(jax.random.fold_in(splits[4], 1), BLOCKS // NB_DEV)
    contact_owner_turns = jax.random.permutation(jax.random.fold_in(splits[4], 3), BLOCKS // NB_DEV)
    contact_owner = jax.vmap(lambda own, number: shared_out(jax.random.fold_in(splits[4], 2), own, number, NB_DEV, N_ROLE * N_DOM, TOPC, CAP, 2))(contact_owner_keys, contact_owner_turns).reshape((BLOCKS, TOPC))
    contact_tile = set_ends(jax.random.randint(splits[5], (BLOCKS, TOPC), 0, TILES_DEV), jax.random.fold_in(splits[5], 1), 0, TILES_DEV - 1).astype(jnp.int32)
    halo_tiles = set_ends(jax.random.randint(splits[6], (N_ROLE * N_DOM * HB,), 0, TILES_DEV), jax.random.fold_in(splits[6], 1), 0, TILES_DEV - 1).astype(jnp.int32)
    block_inverse = draw_block_inverse(jax.random.fold_in(splits[10], 71), 0)
    pattern = set_ends(jax.random.randint(splits[8], (BLOCKS, NNZB), 0, NB_DEV), jax.random.fold_in(splits[8], 1), 0, NB_DEV - 1).astype(jnp.int32)
    coupling = jnp.clip(0.05 + 0.15 * jax.random.uniform(splits[9], (BLOCKS, NNZB), jnp.float32) ** block_levels(splits[9], (BLOCKS, NNZB), ((0, 128),), -0.2, 0.2), 0.05, 0.2)
    return dict(tire_pos=tire_pos, tire_vel=tire_vel, part_pos=part_pos, part_vel=part_vel, contact_owner=contact_owner, contact_tile=contact_tile, halo_tiles=halo_tiles, block_inverse=block_inverse, pattern=pattern, coupling=coupling)


contact_gain = 0.05
soil_gain = 0.05
time_step = 0.1
spread_sq = 4.0


def pair_force(near_pos, far_pos, gain, live):
    diff = near_pos[:, :, :, None] - far_pos[:, :, None, :]
    dist = jnp.sum(diff * diff, axis=1)
    weight = gain * jnp.exp(-dist / spread_sq) * live[:, None, None]
    on_near = jnp.einsum('nij,ncj->nci', weight, far_pos, precision=lax.Precision.HIGHEST)
    on_far = jnp.einsum('nij,nci->ncj', weight, near_pos, precision=lax.Precision.HIGHEST)
    push = near_pos * jnp.sum(weight, axis=2)[:, None, :] - on_near
    react = far_pos * jnp.sum(weight, axis=1)[:, None, :] - on_far
    return push, react


def reference(tire_pos, tire_vel, part_pos, part_vel, contact_owner, contact_tile, halo_tiles, block_inverse, pattern, coupling):
    devices = N_ROLE * N_DOM
    total_tiles = TILES_DEV * devices
    pairs = BLOCKS * TOPC
    group = 64
    pair_block = jnp.arange(pairs, dtype=jnp.int32) // TOPC
    pair_tile = (contact_owner * TILES_DEV + contact_tile).reshape(-1).astype(jnp.int32)
    dom_index = jnp.arange(devices, dtype=jnp.int32)
    own_tile = (dom_index[:, None] * TILES_DEV + halo_tiles.reshape(devices, HB))[1:].reshape(-1)
    src_tile = (dom_index[:, None] * TILES_DEV + halo_tiles.reshape(devices, HB))[:-1].reshape(-1)
    glob_pattern = (jnp.arange(BLOCKS, dtype=jnp.int32) // NB_DEV)[:, None] * NB_DEV + pattern
    for step_count in range(STEPS):
        node_blocks = tire_pos.reshape(3, BLOCKS, BLK).transpose(1, 0, 2)
        part_tiles = part_pos.reshape(3, total_tiles, BLK).transpose(1, 0, 2)
        near_all = node_blocks[pair_block].reshape(pairs // group, group, 3, BLK)
        far_all = part_tiles[pair_tile].reshape(pairs // group, group, 3, BLK)

        def one_group(items):
            return pair_force(items[0], items[1], contact_gain, jnp.ones((group,), jnp.float32))

        push, react = lax.map(one_group, (near_all, far_all))
        node_force = push.reshape(BLOCKS, TOPC, 3, BLK).sum(axis=1)
        soil_force = jax.ops.segment_sum(react.reshape(pairs, 3, BLK), pair_tile, total_tiles)
        halo_push, unused = pair_force(part_tiles[own_tile], part_tiles[src_tile], soil_gain, jnp.ones((own_tile.shape[0],), jnp.float32))
        soil_force = soil_force + jax.ops.segment_sum(halo_push, own_tile, total_tiles)
        soil_flat = soil_force.transpose(1, 0, 2).reshape(3, -1)
        vel_blocks = tire_vel.reshape(3, BLOCKS, BLK).transpose(1, 0, 2)
        rhs = vel_blocks + time_step * node_force
        velocity = jnp.einsum('bij,bcj->bci', block_inverse, rhs, precision=lax.Precision.HIGHEST)
        for sweep_count in range(SWEEPS):
            coupled = rhs + jnp.sum(coupling[:, :, None, None] * velocity[glob_pattern], axis=1)
            velocity = jnp.einsum('bij,bcj->bci', block_inverse, coupled, precision=lax.Precision.HIGHEST)
        part_vel = part_vel + time_step * soil_flat
        part_pos = part_pos + time_step * part_vel
        tire_vel = velocity.transpose(1, 0, 2).reshape(3, -1)
        tire_pos = tire_pos + time_step * tire_vel
    return tire_pos, tire_vel, part_pos, part_vel
```

```python
import functools
import math

import jax
import jax.numpy as jnp
from jax import lax
from jax.experimental import pallas as pl
from jax.experimental.pallas import tpu as pltpu
from jax.sharding import PartitionSpec as P

BLK = 128
TOPC = 2
NNZB = 3
SWEEPS = 3
HB = 4
GROUP = 16
UNROLL = 8

BF = jnp.bfloat16
F32 = jnp.float32
MESH = pl.DeviceIdType.MESH

gain = 0.05
time_step = 0.1
spread_sq = 4.0
SCALE = math.sqrt(2.0 * math.log2(math.e) / spread_sq)


def split2(x):
    hi = x.astype(BF).astype(F32)
    return hi, x - hi


def split3(x):
    hi = x.astype(BF).astype(F32)
    rest = x - hi
    mid = rest.astype(BF).astype(F32)
    return hi, mid, rest - mid


def dot(a, b):
    return jnp.dot(a, b, preferred_element_type=F32)


def dot_nt(a, b):
    return lax.dot_general(a, b, (((1,), (1,)), ((), ())), preferred_element_type=F32)


def dot_tn(a, b):
    return lax.dot_general(a, b, (((0,), (0,)), ((), ())), preferred_element_type=F32)


def pair(near, far):
    row = lax.broadcasted_iota(jnp.int32, (8, BLK), 0)
    near_s = near * SCALE
    far_s = far * SCALE

    def norms(t):
        sq = t * t * (-0.5)
        first = jnp.sum(jnp.where(row < 3, sq, 0.0), axis=0, keepdims=True)
        second = jnp.sum(
            jnp.where((row >= 3) & (row < 6), sq, 0.0), axis=0, keepdims=True
        )
        return first, second

    nx0, nx1 = norms(near_s)
    ny = norms(far_s)
    xh, xm, xl = split3(jnp.where(row < 6, near_s, jnp.where(row == 6, nx0, nx1)))
    one = jnp.ones((8, BLK), F32)
    lhs = jnp.concatenate([xh, xm, xl, xh, xm, xh, one, one], axis=0).astype(BF)
    yh, ym, yl = split3(jnp.where(row < 6, far_s, 0.0))
    sides = []
    for k in range(2):
        mask = (row >= 3 * k) & (row < 3 * k + 3)

        def keep(t):
            return jnp.where(mask, t, 0.0)

        yhk = keep(yh) + (row == 6 + k).astype(F32)
        nh, nm, nl = split3(ny[k])
        nrows = jnp.where(
            row == 0, nh, jnp.where(row == 1, nm, jnp.where(row == 2, nl, 0.0))
        )
        sides.append(
            jnp.concatenate(
                [yhk, yhk, yhk, keep(ym), keep(ym), keep(yl), nrows, one * 0.0], axis=0
            )
        )
    rhs = jnp.concatenate(sides, axis=1).astype(BF)
    weight = jnp.exp2(jnp.minimum(dot_tn(lhs, rhs), 0.0))
    w_hi = weight.astype(BF)
    w_lo = (weight - w_hi.astype(F32)).astype(BF)
    h0, h1 = w_hi[:, :BLK], w_hi[:, BLK:]
    l0, l1 = w_lo[:, :BLK], w_lo[:, BLK:]

    def features(t):
        h, l = split2(t)
        h = jnp.where(row == 6, 1.0, jnp.where(row == 7, 0.0, h))
        l = jnp.where(row < 6, l, 0.0)
        a = jnp.concatenate([h, l], axis=0).astype(BF)
        return jnp.concatenate([a, a], axis=1)

    over_near = jnp.concatenate([w_hi, w_lo], axis=0)
    over_far = jnp.concatenate(
        [jnp.concatenate([h0, l0], axis=1), jnp.concatenate([h1, l1], axis=1)], axis=0
    )
    sum_near = dot(features(near), over_near)
    sum_far = dot_nt(features(far), over_far)

    def force(t, o):
        a = o[0:8, :BLK] + o[8:16, :BLK]
        b = o[0:8, BLK:] + o[8:16, BLK:]
        total = jnp.where(row < 3, a[6:7, :], b[6:7, :])
        return gain * (t * total - jnp.where(row < 3, a, b))

    return force(near, sum_far), force(far, sum_near)


def kernel(
    n,
    n_dom,
    nb,
    nt,
    tire_pos,
    tire_vel,
    part_pos,
    part_vel,
    owner,
    ctile,
    halo,
    binv,
    pattern,
    coup,
    o_tp,
    o_tv,
    o_pp,
    o_pv,
    bstage,
    bsplit,
    nscr,
    pscr,
    send1,
    near1,
    far1,
    push1,
    pret,
    react1,
    tsend,
    tret,
    near2,
    push2,
    react2,
    rret,
    edge,
    hrecv,
    hpush,
    vs,
    vo,
    tst,
    sk_t,
    sk_n,
    oh_n,
    oh_t,
    bsem,
    ssem,
    rsem1,
    psem,
    tsem,
    rrsem,
    hsem,
    hssem,
):
    me = lax.axis_index("role") * n_dom + lax.axis_index("dom")

    def dev(p):
        return (p // n_dom, p % n_dom)

    def ahead(i):
        return dev((me + i) % n)

    def behind(i):
        return dev((me + n - i) % n)

    barrier = pltpu.get_barrier_semaphore()

    def greet(i, c):
        pl.semaphore_signal(barrier, inc=1, device_id=ahead(i), device_id_type=MESH)
        return c

    lax.fori_loop(1, n, greet, 0)

    bcopy = pltpu.make_async_copy(binv, bstage, bsem)
    bcopy.start()

    def tile_rows(i, rows=8):
        return pl.ds(pl.multiple_of(i * 8, 8), rows)

    def comps(ref, count, first=0):
        return [ref[pl.ds(first + c, count, stride=8), :] for c in range(3)]

    def put(ref, count, vals, first=0):
        for c in range(len(vals)):
            ref[pl.ds(first + c, count, stride=8), :] = vals[c]

    def spread(src, scr, count):
        for b in range(count):
            scr[b * 8 : b * 8 + 3, :] = src[:, b * BLK : (b + 1) * BLK]

    def collect(scr, dst, count):
        for b in range(count):
            dst[:, b * BLK : (b + 1) * BLK] = scr[b * 8 : b * 8 + 3, :]

    lane = lax.broadcasted_iota(jnp.int32, (BLK, BLK), 1)
    sub = lax.broadcasted_iota(jnp.int32, (BLK, BLK), 0)

    def pad_rows(x, rows=BLK):
        if x.shape[0] == rows:
            return x
        return jnp.concatenate(
            [x, jnp.zeros((rows - x.shape[0], x.shape[1]), x.dtype)], axis=0
        )

    lane_b = lax.broadcasted_iota(jnp.int32, (nb, BLK), 1)
    hot = jnp.zeros((nb, BLK), F32)
    tile_of = jnp.zeros((nb, BLK), F32)
    for m in range(TOPC):
        rel = (owner[:, m : m + 1] - me + n) & (n - 1)
        is_m = lane_b == rel
        hot = hot + jnp.where(is_m, 1.0, 0.0)
        tile_of = tile_of + jnp.where(
            is_m, (ctile[:, m : m + 1] + 1).astype(F32), 0.0
        )
    hot_p = pad_rows(hot)
    lower = jnp.where(lane < sub, 1.0, 0.0).astype(BF)
    rank = dot(lower, hot_p.astype(BF))
    tile_p = pad_rows(tile_of)
    ids = []
    for k in range(2):
        u = jnp.where((hot_p > 0.5) & (jnp.abs(rank - k) < 0.5), tile_p, 0.0)
        ut = jnp.transpose(u)
        sk_t[k] = jnp.where(u > 0.5, 1.0, 0.0).astype(BF)
        sk_n[k] = jnp.where(ut > 0.5, 1.0, 0.0).astype(BF)
        ids.append(jnp.sum(ut, axis=1, keepdims=True) - 1.0)

    def node_slots(x, dst):
        cat = jnp.concatenate(x, axis=1)
        parts = [pad_rows(t.astype(BF)) for t in split3(cat)]
        for k in range(2):
            g = dot(sk_n[k], parts[0]) + dot(sk_n[k], parts[1]) + dot(sk_n[k], parts[2])
            put(dst, n, [g[:, c * BLK : (c + 1) * BLK] for c in range(3)], 3 * k)

    spread(tire_pos, nscr, nb)
    tp = comps(nscr, nb)
    node_slots(tp, send1)
    send1[pl.ds(6, n, stride=8), :] = jnp.where(
        lane < nt, jnp.broadcast_to(ids[0], (n, BLK)), jnp.broadcast_to(ids[1], (n, BLK))
    )

    pl.semaphore_wait(barrier, n - 1)

    def wait_rows(ref, sem, count, rows):
        view = ref.at[pl.ds(0, count * rows), :]
        pltpu.make_async_copy(view, view, sem).wait()

    def remote(src, dst, i, rows, sem_s, sem_r, target):
        pltpu.make_async_remote_copy(
            src_ref=src.at[tile_rows(i, rows), :],
            dst_ref=dst.at[tile_rows(i, rows), :],
            send_sem=sem_s,
            recv_sem=sem_r,
            device_id=target,
            device_id_type=MESH,
        ).start()

    def own(src, dst, rows, sem_r):
        pltpu.make_async_copy(
            src.at[pl.ds(0, rows), :], dst.at[pl.ds(0, rows), :], sem_r
        ).start()

    own(send1, near1, 7, rsem1.at[0])

    def send_pos(i, c):
        remote(send1, near1, i, 7, ssem.at[0], rsem1.at[i // GROUP], ahead(i))
        return c

    lax.fori_loop(1, n, send_pos, 0)

    def tiles_split(x):
        cat = jnp.concatenate(x, axis=1)
        for s, t in enumerate(split3(cat)):
            t = t.astype(BF)
            tst[s, 0:nt, :] = t
            tst[s, nt : 2 * nt, :] = t

    def send_edges(step):
        for u in range(2):
            a = pscr[pl.ds(halo[2 * u] * 8, 8), :]
            b = pscr[pl.ds(halo[2 * u + 1] * 8, 8), :]
            edge[pl.ds((2 * step + u) * 8, 8), :] = jnp.concatenate(
                [a[0:3], b[0:3], jnp.zeros((2, BLK), F32)], axis=0
            )
        pltpu.make_async_remote_copy(
            src_ref=edge.at[pl.ds(step * 16, 16), :],
            dst_ref=hrecv.at[pl.ds(step * 16, 16), :],
            send_sem=hssem.at[step],
            recv_sem=hsem.at[step],
            device_id=ahead(1),
            device_id_type=MESH,
        ).start()

    spread(part_pos, pscr, nt)
    pp = comps(pscr, nt)
    tiles_split(pp)
    send_edges(0)

    live = jnp.where(me > 0, 1.0, 0.0).astype(F32)
    sub_t = lax.broadcasted_iota(jnp.int32, (nt, BLK), 0)

    def halo_force(step):
        view = hrecv.at[pl.ds(step * 16, 16), :]
        pltpu.make_async_copy(view, view, hsem.at[step]).wait()
        out = [jnp.zeros((nt, BLK), F32) for _ in range(3)]
        for u in range(2):
            at = pl.ds((2 * step + u) * 8, 8)
            force, unused = pair(edge[at, :], hrecv[at, :])
            force = force * live
            for k in range(2):
                here = sub_t == halo[2 * u + k]
                for c in range(3):
                    r = 3 * k + c
                    out[c] = out[c] + jnp.where(here, force[r : r + 1, :], 0.0)
        return out

    bcopy.wait()

    def split_block(q, c):
        for s in range(2):
            b = bstage[2 * q + s]
            hi = b.astype(BF)
            bsplit[q, s * BLK : (s + 1) * BLK, 0:BLK] = hi
            bsplit[q, s * BLK : (s + 1) * BLK, BLK : 2 * BLK] = (
                b - hi.astype(F32)
            ).astype(BF)
        return c

    lax.fori_loop(0, nb // 2, split_block, 0)

    cmat = jnp.zeros((nb, BLK), F32)
    for m in range(NNZB):
        cmat = cmat + jnp.where(lane_b == pattern[:, m : m + 1], coup[:, m : m + 1], 0.0)
    c_hi = cmat.astype(BF)
    c_lo = (cmat - c_hi.astype(F32)).astype(BF)
    vs[...] = jnp.zeros_like(vs)

    def matvec(x):
        for c in range(3):
            h, l = split2(x[c])
            vs[pl.ds(c, nb, stride=8), :] = h
            vs[pl.ds(3 + c, nb, stride=8), :] = l

        def some(j, carry):
            for u in range(UNROLL):
                q = j * UNROLL + u
                at = pl.ds(pl.multiple_of(q * 16, 16), 16)
                t = vs[at, :].astype(BF)
                o = dot_nt(jnp.concatenate([t, t], axis=1), bsplit[q])
                vo[at, :] = jnp.concatenate([o[0:8, :BLK], o[8:16, BLK:]], axis=0)
            return carry

        lax.fori_loop(0, nb // 2 // UNROLL, some, 0)
        a, b = comps(vo, nb), comps(vo, nb, 3)
        return [a[c] + b[c] for c in range(3)]

    def couple(v):
        h, l = split2(jnp.concatenate(v, axis=1))
        h, l = pad_rows(h.astype(BF)), pad_rows(l.astype(BF))
        o = dot(c_hi, h) + dot(c_lo, h) + dot(c_hi, l)
        return [o[:, c * BLK : (c + 1) * BLK] for c in range(3)]

    def solve(rhs):
        v = matvec(rhs)
        for _ in range(SWEEPS):
            w = couple(v)
            v = matvec([rhs[c] + w[c] for c in range(3)])
        return v

    def by_slot(ref, k):
        return jnp.concatenate(comps(ref, n, 3 * k), axis=1)

    def gather_sum(mats, ref):
        total = None
        for k in range(2):
            h, l = split2(by_slot(ref, k))
            o = dot(mats[k], h.astype(BF)) + dot(mats[k], l.astype(BF))
            total = o if total is None else total + o
        return [total[:, c * BLK : (c + 1) * BLK] for c in range(3)]

    def soil_sum(ref):
        return gather_sum([oh_t[0:nt, :], oh_t[nt : 2 * nt, :]], ref)

    def node_sum(ref):
        return gather_sum([sk_t[0, 0:nb, :], sk_t[1, 0:nb, :]], ref)

    lane_g = lax.broadcasted_iota(jnp.int32, (GROUP, BLK), 1)
    lane_gm = (lane_g & (nt - 1)).astype(F32)

    def owner_group(g, c):
        base = pl.multiple_of(g * GROUP * 8, GROUP * 8)
        wait_rows(near1, rsem1.at[g], GROUP, 7)
        tid = near1[pl.ds(base + 6, GROUP, stride=8), :]
        oh = jnp.where(tid == lane_gm, 1.0, 0.0)
        sel = jnp.concatenate(
            [jnp.where(lane_g < nt, oh, 0.0), jnp.where(lane_g < nt, 0.0, oh)], axis=0
        ).astype(BF)
        got = dot(sel, tst[0]) + dot(sel, tst[1]) + dot(sel, tst[2])
        for k in range(2):
            for cc in range(3):
                far1[pl.ds(base + 3 * k + cc, GROUP, stride=8), :] = got[
                    k * GROUP : (k + 1) * GROUP, cc * BLK : (cc + 1) * BLK
                ]

        def some(j, carry):
            for u in range(UNROLL):
                i = g * GROUP + j * UNROLL + u
                at = tile_rows(i)
                push1[at, :], react1[at, :] = pair(near1[at, :], far1[at, :])
            for u in range(UNROLL):
                i = g * GROUP + j * UNROLL + u

                @pl.when(i > 0)
                def _():
                    remote(push1, pret, i, 6, ssem.at[1], psem, behind(i))

                @pl.when(i == 0)
                def _():
                    own(push1, pret, 6, psem)

            return carry

        lax.fori_loop(0, GROUP // UNROLL, some, 0)
        return c

    lax.fori_loop(0, n // GROUP, owner_group, 0)

    lane_m = (lane & (nt - 1)).astype(F32)
    oh_all = jnp.where(near1[pl.ds(6, n, stride=8), :] == lane_m, 1.0, 0.0)
    oh_n[0] = jnp.where(lane < nt, oh_all, 0.0).astype(BF)
    oh_n[1] = jnp.where(lane < nt, 0.0, oh_all).astype(BF)
    oh_t[...] = jnp.transpose(oh_all).astype(BF)

    hf = halo_force(0)
    sf = soil_sum(react1)
    spread(part_vel, pscr, nt)
    pv = comps(pscr, nt)
    pv = [pv[c] + time_step * (sf[c] + hf[c]) for c in range(3)]
    pp = [pp[c] + time_step * pv[c] for c in range(3)]
    put(pscr, nt, pp)
    tiles_split(pp)
    for k in range(2):
        got = dot(oh_n[k], tst[0]) + dot(oh_n[k], tst[1]) + dot(oh_n[k], tst[2])
        put(tsend, n, [got[:, c * BLK : (c + 1) * BLK] for c in range(3)], 3 * k)

    own(tsend, tret, 6, tsem.at[0])

    def send_tiles(i, c):
        remote(tsend, tret, i, 6, ssem.at[2], tsem.at[i // GROUP], behind(i))
        return c

    lax.fori_loop(1, n, send_tiles, 0)
    send_edges(1)

    spread(tire_vel, nscr, nb)
    tv = comps(nscr, nb)
    wait_rows(pret, psem, n, 6)
    nf = node_sum(pret)
    tv = solve([tv[c] + time_step * nf[c] for c in range(3)])
    tp = [tp[c] + time_step * tv[c] for c in range(3)]
    node_slots(tp, near2)

    def node_group(g, c):
        wait_rows(tret, tsem.at[g], GROUP, 6)

        def some(j, carry):
            for u in range(UNROLL):
                i = g * GROUP + j * UNROLL + u
                at = tile_rows(i)
                push2[at, :], react2[at, :] = pair(near2[at, :], tret[at, :])
            for u in range(UNROLL):
                i = g * GROUP + j * UNROLL + u

                @pl.when(i > 0)
                def _():
                    remote(react2, rret, i, 6, ssem.at[3], rrsem, ahead(i))

                @pl.when(i == 0)
                def _():
                    own(react2, rret, 6, rrsem)

            return carry

        lax.fori_loop(0, GROUP // UNROLL, some, 0)
        return c

    lax.fori_loop(0, n // GROUP, node_group, 0)

    nf = node_sum(push2)
    tv = solve([tv[c] + time_step * nf[c] for c in range(3)])
    tp = [tp[c] + time_step * tv[c] for c in range(3)]
    put(nscr, nb, tv)
    collect(nscr, o_tv, nb)
    put(nscr, nb, tp)
    collect(nscr, o_tp, nb)

    hf = halo_force(1)
    wait_rows(rret, rrsem, n, 6)
    sf = soil_sum(rret)
    pv = [pv[c] + time_step * (sf[c] + hf[c]) for c in range(3)]
    pp = [pp[c] + time_step * pv[c] for c in range(3)]
    put(pscr, nt, pv)
    collect(pscr, o_pv, nt)
    put(pscr, nt, pp)
    collect(pscr, o_pp, nt)

    wait_rows(send1, ssem.at[0], n - 1, 7)
    for s in range(1, 4):
        wait_rows(push1, ssem.at[s], n - 1, 6)
    for step in range(2):
        view = edge.at[pl.ds(step * 16, 16), :]
        pltpu.make_async_copy(view, view, hssem.at[step]).wait()


def local(
    n,
    n_dom,
    tire_pos,
    tire_vel,
    part_pos,
    part_vel,
    contact_owner,
    contact_tile,
    halo_tiles,
    block_inverse,
    pattern,
    coupling,
):
    nb = tire_pos.shape[1] // BLK
    nt = part_pos.shape[1] // BLK
    vmem = pl.BlockSpec(memory_space=pltpu.VMEM)
    smem = pl.BlockSpec(memory_space=pltpu.SMEM)
    hbm = pl.BlockSpec(memory_space=pl.ANY)
    message = pltpu.VMEM((n * 8, BLK), F32)
    return pl.pallas_call(
        functools.partial(kernel, n, n_dom, nb, nt),
        out_shape=(
            jax.ShapeDtypeStruct(tire_pos.shape, F32),
            jax.ShapeDtypeStruct(tire_pos.shape, F32),
            jax.ShapeDtypeStruct(part_pos.shape, F32),
            jax.ShapeDtypeStruct(part_pos.shape, F32),
        ),
        in_specs=[vmem, vmem, vmem, vmem, vmem, vmem, smem, hbm, vmem, vmem],
        out_specs=[vmem] * 4,
        scratch_shapes=[
            pltpu.VMEM((nb, BLK, BLK), F32),
            pltpu.VMEM((nb // 2, 2 * BLK, 2 * BLK), BF),
            pltpu.VMEM((nb * 8, BLK), F32),
            pltpu.VMEM((nt * 8, BLK), F32),
        ]
        + [message] * 12
        + [
            pltpu.VMEM((32, BLK), F32),
            pltpu.VMEM((32, BLK), F32),
            pltpu.VMEM((16, BLK), F32),
            pltpu.VMEM((nb * 8, BLK), F32),
            pltpu.VMEM((nb * 8, BLK), F32),
            pltpu.VMEM((3, 2 * nt, 3 * BLK), BF),
            pltpu.VMEM((2, BLK, BLK), BF),
            pltpu.VMEM((2, BLK, BLK), BF),
            pltpu.VMEM((2, BLK, BLK), BF),
            pltpu.VMEM((BLK, BLK), BF),
            pltpu.SemaphoreType.DMA,
            pltpu.SemaphoreType.DMA((4,)),
            pltpu.SemaphoreType.DMA((n // GROUP,)),
            pltpu.SemaphoreType.DMA,
            pltpu.SemaphoreType.DMA((n // GROUP,)),
            pltpu.SemaphoreType.DMA,
            pltpu.SemaphoreType.DMA((2,)),
            pltpu.SemaphoreType.DMA((2,)),
        ],
        compiler_params=pltpu.CompilerParams(
            collective_id=0, has_side_effects=True, vmem_limit_bytes=48 << 20
        ),
    )(
        tire_pos,
        tire_vel,
        part_pos,
        part_vel,
        contact_owner,
        contact_tile,
        halo_tiles,
        block_inverse,
        pattern,
        coupling,
    )


def solution(mesh):
    n_role, n_dom = mesh.shape["role"], mesh.shape["dom"]
    both = ("role", "dom")
    return jax.shard_map(
        functools.partial(local, n_role * n_dom, n_dom),
        mesh=mesh,
        in_specs=(
            P(None, both),
            P(None, both),
            P(None, both),
            P(None, both),
            P(both, None),
            P(both, None),
            P(both),
            P(both, None, None),
            P(both, None),
            P(both, None),
        ),
        out_specs=(P(None, both), P(None, both), P(None, both), P(None, both)),
        check_vma=False,
    )
```

```python
import functools
import math

import jax
import jax.numpy as jnp
from jax import lax
from jax.experimental import pallas as pl
from jax.experimental.pallas import tpu as pltpu
from jax.sharding import PartitionSpec as P

BLK = 128
TOPC = 2
NNZB = 3
SWEEPS = 3
HB = 4
GROUP = 16
UNROLL = 16

BF = jnp.bfloat16
F32 = jnp.float32
MESH = pl.DeviceIdType.MESH

gain = 0.05
time_step = 0.1
spread_sq = 4.0
SCALE = math.sqrt(2.0 * math.log2(math.e) / spread_sq)


def split2(x):
    hi = x.astype(BF).astype(F32)
    return hi, x - hi


def split3(x):
    hi = x.astype(BF).astype(F32)
    rest = x - hi
    mid = rest.astype(BF).astype(F32)
    return hi, mid, rest - mid


def dot(a, b):
    return jnp.dot(a, b, preferred_element_type=F32)


def dot_nt(a, b):
    return lax.dot_general(a, b, (((1,), (1,)), ((), ())), preferred_element_type=F32)


def dot_tn(a, b):
    return lax.dot_general(a, b, (((0,), (0,)), ((), ())), preferred_element_type=F32)


def pair_weights(near, far):
    row = lax.broadcasted_iota(jnp.int32, (8, BLK), 0)
    near_s = near * SCALE
    far_s = far * SCALE

    def norms(t):
        sq = t * t * (-0.5)
        first = jnp.sum(jnp.where(row < 3, sq, 0.0), axis=0, keepdims=True)
        second = jnp.sum(
            jnp.where((row >= 3) & (row < 6), sq, 0.0), axis=0, keepdims=True
        )
        return first, second

    nx0, nx1 = norms(near_s)
    ny = norms(far_s)
    xh, xm, xl = split3(jnp.where(row < 6, near_s, jnp.where(row == 6, nx0, nx1)))
    one = jnp.ones((8, BLK), F32)
    lhs = jnp.concatenate([xh, xm, xl, xh, xm, xh, one, one], axis=0).astype(BF)
    yh, ym, yl = split3(jnp.where(row < 6, far_s, 0.0))
    sides = []
    for k in range(2):
        mask = (row >= 3 * k) & (row < 3 * k + 3)

        def keep(t):
            return jnp.where(mask, t, 0.0)

        yhk = keep(yh) + (row == 6 + k).astype(F32)
        nh, nm, nl = split3(ny[k])
        nrows = jnp.where(
            row == 0, nh, jnp.where(row == 1, nm, jnp.where(row == 2, nl, 0.0))
        )
        sides.append(
            jnp.concatenate(
                [yhk, yhk, yhk, keep(ym), keep(ym), keep(yl), nrows, one * 0.0], axis=0
            )
        )
    rhs = jnp.concatenate(sides, axis=1).astype(BF)
    weight = jnp.exp2(jnp.minimum(dot_tn(lhs, rhs), 0.0))
    w_hi = weight.astype(BF)
    return w_hi, (weight - w_hi.astype(F32)).astype(BF)


def features(t):
    row = lax.broadcasted_iota(jnp.int32, (8, BLK), 0)
    h, l = split2(t)
    h = jnp.where(row == 6, 1.0, jnp.where(row == 7, 0.0, h))
    l = jnp.where(row < 6, l, 0.0)
    return jnp.concatenate([h, l], axis=0).astype(BF)


def force(t, a, b):
    row = lax.broadcasted_iota(jnp.int32, (8, BLK), 0)
    a = a[0:8] + a[8:16]
    b = b[0:8] + b[8:16]
    total = jnp.where(row < 3, a[6:7, :], b[6:7, :])
    return gain * (t * total - jnp.where(row < 3, a, b))


def put_weights(ws, u, near, far):
    ws[u, 0:BLK, :], ws[u, BLK : 2 * BLK, :] = pair_weights(near, far)


def react_of(ws, u, near, far):
    f = features(near)
    o = dot(jnp.concatenate([f, f], axis=1), ws[u])
    return force(far, o[:, :BLK], o[:, BLK:])


def push_of(ws, u, near, far):
    f = features(far)
    a = dot_nt(f, ws[u, :, :BLK])
    b = dot_nt(f, ws[u, :, BLK:])
    return force(near, a[:, :BLK] + a[:, BLK:], b[:, :BLK] + b[:, BLK:])


def kernel(
    n,
    n_dom,
    nb,
    nt,
    tire_pos,
    tire_vel,
    part_pos,
    part_vel,
    owner,
    ctile,
    halo,
    binv,
    pattern,
    coup,
    o_tp,
    o_tv,
    o_pp,
    o_pv,
    s_tp,
    s_tv,
    s_pp,
    s_pv,
    s_owner,
    s_ctile,
    s_halo,
    s_pattern,
    s_coup,
    ws,
    bstage,
    bsplit,
    nscr,
    pscr,
    send1,
    near1,
    far1,
    push1,
    pret,
    react1,
    tsend,
    tret,
    near2,
    push2,
    react2,
    rret,
    edge,
    hrecv,
    hpush,
    vs,
    vo,
    tst,
    sk_t,
    sk_n,
    oh_n,
    oh_t,
    insem,
    bsem,
    ssem,
    rsem1,
    psem,
    tsem,
    rrsem,
    hsem,
    hssem,
):
    me = lax.axis_index("role") * n_dom + lax.axis_index("dom")

    def dev(p):
        return (p // n_dom, p % n_dom)

    def ahead(i):
        return dev((me + i) % n)

    def behind(i):
        return dev((me + n - i) % n)

    arrive = []
    for k, (src, dst) in enumerate(
        [
            (tire_pos, s_tp),
            (owner, s_owner),
            (ctile, s_ctile),
            (part_pos, s_pp),
            (halo, s_halo),
            (part_vel, s_pv),
            (tire_vel, s_tv),
            (pattern, s_pattern),
            (coup, s_coup),
        ]
    ):
        arrive.append(pltpu.make_async_copy(src, dst, insem.at[k]))
        arrive[k].start()

    def ready(first, last):
        for k in range(first, last):
            arrive[k].wait()

    barrier = pltpu.get_barrier_semaphore()

    def greet(i, c):
        pl.semaphore_signal(barrier, inc=1, device_id=ahead(i), device_id_type=MESH)
        return c

    lax.fori_loop(1, n, greet, 0)

    bcopy = pltpu.make_async_copy(binv, bstage, bsem)
    bcopy.start()

    def tile_rows(i, rows=8):
        return pl.ds(pl.multiple_of(i * 8, 8), rows)

    def comps(ref, count, first=0):
        return [ref[pl.ds(first + c, count, stride=8), :] for c in range(3)]

    def put(ref, count, vals, first=0):
        for c in range(len(vals)):
            ref[pl.ds(first + c, count, stride=8), :] = vals[c]

    def spread(src, scr, count):
        for b in range(count):
            scr[b * 8 : b * 8 + 3, :] = src[:, b * BLK : (b + 1) * BLK]

    def collect(scr, dst, count):
        for b in range(count):
            dst[:, b * BLK : (b + 1) * BLK] = scr[b * 8 : b * 8 + 3, :]

    lane = lax.broadcasted_iota(jnp.int32, (BLK, BLK), 1)
    sub = lax.broadcasted_iota(jnp.int32, (BLK, BLK), 0)

    def pad_rows(x, rows=BLK):
        if x.shape[0] == rows:
            return x
        return jnp.concatenate(
            [x, jnp.zeros((rows - x.shape[0], x.shape[1]), x.dtype)], axis=0
        )

    ready(0, 3)
    sub_b = lax.broadcasted_iota(jnp.int32, (BLK, nb), 0)
    hot = jnp.zeros((BLK, nb), F32)
    tile_of = jnp.zeros((BLK, nb), F32)
    for m in range(TOPC):
        rel = (s_owner[m : m + 1, :] - me + n) & (n - 1)
        is_m = sub_b == rel
        hot = hot + jnp.where(is_m, 1.0, 0.0)
        tile_of = tile_of + jnp.where(
            is_m, (s_ctile[m : m + 1, :] + 1).astype(F32), 0.0
        )

    def pad_lanes(x):
        return jnp.concatenate([x, jnp.zeros((BLK, BLK - nb), x.dtype)], axis=1)

    hot_p = pad_lanes(hot)
    upper = jnp.where(sub < lane, 1.0, 0.0).astype(BF)
    rank = dot(hot_p.astype(BF), upper)
    tile_p = pad_lanes(tile_of)
    ids = []
    for k in range(2):
        u = jnp.where((hot_p > 0.5) & (jnp.abs(rank - k) < 0.5), tile_p, 0.0)
        sk_n[k] = jnp.where(u > 0.5, 1.0, 0.0).astype(BF)
        ids.append(jnp.sum(u, axis=1, keepdims=True) - 1.0)

    def node_slots(x, dst):
        cat = jnp.concatenate(x, axis=1)
        parts = [pad_rows(t.astype(BF)) for t in split3(cat)]
        for k in range(2):
            g = dot(sk_n[k], parts[0]) + dot(sk_n[k], parts[1]) + dot(sk_n[k], parts[2])
            put(dst, n, [g[:, c * BLK : (c + 1) * BLK] for c in range(3)], 3 * k)

    spread(s_tp, nscr, nb)
    tp = comps(nscr, nb)
    node_slots(tp, send1)
    send1[pl.ds(6, n, stride=8), :] = jnp.where(
        lane < nt, jnp.broadcast_to(ids[0], (n, BLK)), jnp.broadcast_to(ids[1], (n, BLK))
    )

    pl.semaphore_wait(barrier, n - 1)

    def wait_rows(ref, sem, count, rows):
        view = ref.at[pl.ds(0, count * rows), :]
        pltpu.make_async_copy(view, view, sem).wait()

    def remote(src, dst, i, rows, sem_s, sem_r, target):
        pltpu.make_async_remote_copy(
            src_ref=src.at[tile_rows(i, rows), :],
            dst_ref=dst.at[tile_rows(i, rows), :],
            send_sem=sem_s,
            recv_sem=sem_r,
            device_id=target,
            device_id_type=MESH,
        ).start()

    def own(src, dst, rows, sem_r):
        pltpu.make_async_copy(
            src.at[pl.ds(0, rows), :], dst.at[pl.ds(0, rows), :], sem_r
        ).start()

    own(send1, near1, 7, rsem1.at[0])

    def send_pos(i, c):
        remote(send1, near1, i, 7, ssem.at[0], rsem1.at[i // GROUP], ahead(i))
        return c

    lax.fori_loop(1, n, send_pos, 0)

    def tiles_split(x):
        cat = jnp.concatenate(x, axis=1)
        for s, t in enumerate(split3(cat)):
            t = t.astype(BF)
            tst[s, 0:nt, :] = t
            tst[s, nt : 2 * nt, :] = t

    def send_edges(step):
        for u in range(2):
            a = pscr[pl.ds(s_halo[2 * u] * 8, 8), :]
            b = pscr[pl.ds(s_halo[2 * u + 1] * 8, 8), :]
            edge[pl.ds((2 * step + u) * 8, 8), :] = jnp.concatenate(
                [a[0:3], b[0:3], jnp.zeros((2, BLK), F32)], axis=0
            )
        pltpu.make_async_remote_copy(
            src_ref=edge.at[pl.ds(step * 16, 16), :],
            dst_ref=hrecv.at[pl.ds(step * 16, 16), :],
            send_sem=hssem.at[step],
            recv_sem=hsem.at[step],
            device_id=ahead(1),
            device_id_type=MESH,
        ).start()

    ready(3, 5)
    spread(s_pp, pscr, nt)
    pp = comps(pscr, nt)
    tiles_split(pp)
    send_edges(0)

    live = jnp.where(me > 0, 1.0, 0.0).astype(F32)
    sub_t = lax.broadcasted_iota(jnp.int32, (nt, BLK), 0)

    def halo_force(step):
        view = hrecv.at[pl.ds(step * 16, 16), :]
        pltpu.make_async_copy(view, view, hsem.at[step]).wait()
        out = [jnp.zeros((nt, BLK), F32) for _ in range(3)]
        for u in range(2):
            at = pl.ds((2 * step + u) * 8, 8)
            put_weights(ws, u, edge[at, :], hrecv[at, :])
            push = push_of(ws, u, edge[at, :], hrecv[at, :]) * live
            for k in range(2):
                here = sub_t == s_halo[2 * u + k]
                for c in range(3):
                    r = 3 * k + c
                    out[c] = out[c] + jnp.where(here, push[r : r + 1, :], 0.0)
        return out

    for k in range(2):
        sk_t[k] = jnp.transpose(sk_n[k].astype(F32)).astype(BF)
    ready(5, 9)
    bcopy.wait()

    def split_block(q, c):
        for s in range(2):
            b = jnp.transpose(bstage[2 * q + s])
            hi = b.astype(BF)
            bsplit[q, 0:BLK, s * BLK : (s + 1) * BLK] = hi
            bsplit[q, BLK : 2 * BLK, s * BLK : (s + 1) * BLK] = (
                b - hi.astype(F32)
            ).astype(BF)
        return c

    lax.fori_loop(0, nb // 2, split_block, 0, unroll=4)

    cmat = jnp.zeros((BLK, nb), F32)
    for m in range(NNZB):
        cmat = cmat + jnp.where(
            sub_b == s_pattern[m : m + 1, :], s_coup[m : m + 1, :], 0.0
        )
    cmat = jnp.transpose(pad_lanes(cmat))[0:nb]
    c_hi = cmat.astype(BF)
    c_lo = (cmat - c_hi.astype(F32)).astype(BF)
    vs[...] = jnp.zeros_like(vs)

    def matvec(x):
        for c in range(3):
            h, l = split2(x[c])
            vs[pl.ds(c, nb, stride=8), :] = h
            vs[pl.ds(3 + c, nb, stride=8), :] = l

        def some(j, carry):
            for u in range(UNROLL):
                q = j * UNROLL + u
                at = pl.ds(pl.multiple_of(q * 16, 16), 16)
                t = vs[at, :].astype(BF)
                o = dot(jnp.concatenate([t, t], axis=1), bsplit[q])
                vo[at, :] = jnp.concatenate([o[0:8, :BLK], o[8:16, BLK:]], axis=0)
            return carry

        lax.fori_loop(0, nb // 2 // UNROLL, some, 0)
        a, b = comps(vo, nb), comps(vo, nb, 3)
        return [a[c] + b[c] for c in range(3)]

    def couple(v):
        h, l = split2(jnp.concatenate(v, axis=1))
        h, l = pad_rows(h.astype(BF)), pad_rows(l.astype(BF))
        o = dot(c_hi, h) + dot(c_lo, h) + dot(c_hi, l)
        return [o[:, c * BLK : (c + 1) * BLK] for c in range(3)]

    def solve(rhs):
        v = matvec(rhs)
        for _ in range(SWEEPS):
            w = couple(v)
            v = matvec([rhs[c] + w[c] for c in range(3)])
        return v

    def by_slot(ref, k):
        return jnp.concatenate(comps(ref, n, 3 * k), axis=1)

    def gather_sum(mats, ref):
        total = None
        for k in range(2):
            h, l = split2(by_slot(ref, k))
            o = dot(mats[k], h.astype(BF)) + dot(mats[k], l.astype(BF))
            total = o if total is None else total + o
        return [total[:, c * BLK : (c + 1) * BLK] for c in range(3)]

    def soil_sum(ref):
        return gather_sum([oh_t[0:nt, :], oh_t[nt : 2 * nt, :]], ref)

    def node_sum(ref):
        return gather_sum([sk_t[0, 0:nb, :], sk_t[1, 0:nb, :]], ref)

    lane_g = lax.broadcasted_iota(jnp.int32, (GROUP, BLK), 1)
    lane_gm = (lane_g & (nt - 1)).astype(F32)

    def pairs(g, near, far, push, react):
        for u in range(GROUP):
            at = tile_rows(g * GROUP + u)
            put_weights(ws, u, near[at, :], far[at, :])
        for u in range(GROUP):
            at = tile_rows(g * GROUP + u)
            react[at, :] = react_of(ws, u, near[at, :], far[at, :])
            push[at, :] = push_of(ws, u, near[at, :], far[at, :])

    def owner_group(g, c):
        base = pl.multiple_of(g * GROUP * 8, GROUP * 8)
        wait_rows(near1, rsem1.at[g], GROUP, 7)
        tid = near1[pl.ds(base + 6, GROUP, stride=8), :]
        oh = jnp.where(tid == lane_gm, 1.0, 0.0)
        sel = jnp.concatenate(
            [jnp.where(lane_g < nt, oh, 0.0), jnp.where(lane_g < nt, 0.0, oh)], axis=0
        ).astype(BF)
        got = dot(sel, tst[0]) + dot(sel, tst[1]) + dot(sel, tst[2])
        for k in range(2):
            for cc in range(3):
                far1[pl.ds(base + 3 * k + cc, GROUP, stride=8), :] = got[
                    k * GROUP : (k + 1) * GROUP, cc * BLK : (cc + 1) * BLK
                ]

        pairs(g, near1, far1, push1, react1)
        for u in range(GROUP):
            i = g * GROUP + u
            if u > 0:
                remote(push1, pret, i, 6, ssem.at[1], psem, behind(i))
            else:

                @pl.when(i > 0)
                def _():
                    remote(push1, pret, i, 6, ssem.at[1], psem, behind(i))

                @pl.when(i == 0)
                def _():
                    own(push1, pret, 6, psem)

        return c

    lax.fori_loop(0, n // GROUP, owner_group, 0)

    lane_m = (lane & (nt - 1)).astype(F32)
    oh_all = jnp.where(near1[pl.ds(6, n, stride=8), :] == lane_m, 1.0, 0.0)
    oh_n[0] = jnp.where(lane < nt, oh_all, 0.0).astype(BF)
    oh_n[1] = jnp.where(lane < nt, 0.0, oh_all).astype(BF)
    oh_t[...] = jnp.transpose(oh_all).astype(BF)

    hf = halo_force(0)
    sf = soil_sum(react1)
    spread(s_pv, pscr, nt)
    pv = comps(pscr, nt)
    pv = [pv[c] + time_step * (sf[c] + hf[c]) for c in range(3)]
    pp = [pp[c] + time_step * pv[c] for c in range(3)]
    put(pscr, nt, pp)
    tiles_split(pp)
    for k in range(2):
        got = dot(oh_n[k], tst[0]) + dot(oh_n[k], tst[1]) + dot(oh_n[k], tst[2])
        put(tsend, n, [got[:, c * BLK : (c + 1) * BLK] for c in range(3)], 3 * k)

    own(tsend, tret, 6, tsem.at[0])

    def send_tiles(i, c):
        remote(tsend, tret, i, 6, ssem.at[2], tsem.at[i // GROUP], behind(i))
        return c

    lax.fori_loop(1, n, send_tiles, 0)
    send_edges(1)

    spread(s_tv, nscr, nb)
    tv = comps(nscr, nb)
    wait_rows(pret, psem, n, 6)
    nf = node_sum(pret)
    tv = solve([tv[c] + time_step * nf[c] for c in range(3)])
    tp = [tp[c] + time_step * tv[c] for c in range(3)]
    node_slots(tp, near2)

    def node_group(g, c):
        wait_rows(tret, tsem.at[g], GROUP, 6)

        pairs(g, near2, tret, push2, react2)
        for u in range(GROUP):
            i = g * GROUP + u
            if u > 0:
                remote(react2, rret, i, 6, ssem.at[3], rrsem, ahead(i))
            else:

                @pl.when(i > 0)
                def _():
                    remote(react2, rret, i, 6, ssem.at[3], rrsem, ahead(i))

                @pl.when(i == 0)
                def _():
                    own(react2, rret, 6, rrsem)

        return c

    lax.fori_loop(0, n // GROUP, node_group, 0)

    nf = node_sum(push2)
    tv = solve([tv[c] + time_step * nf[c] for c in range(3)])
    tp = [tp[c] + time_step * tv[c] for c in range(3)]
    put(nscr, nb, tv)
    collect(nscr, o_tv, nb)
    put(nscr, nb, tp)
    collect(nscr, o_tp, nb)

    hf = halo_force(1)
    wait_rows(rret, rrsem, n, 6)
    sf = soil_sum(rret)
    pv = [pv[c] + time_step * (sf[c] + hf[c]) for c in range(3)]
    pp = [pp[c] + time_step * pv[c] for c in range(3)]
    put(pscr, nt, pv)
    collect(pscr, o_pv, nt)
    put(pscr, nt, pp)
    collect(pscr, o_pp, nt)

    wait_rows(send1, ssem.at[0], n - 1, 7)
    for s in range(1, 4):
        wait_rows(push1, ssem.at[s], n - 1, 6)
    for step in range(2):
        view = edge.at[pl.ds(step * 16, 16), :]
        pltpu.make_async_copy(view, view, hssem.at[step]).wait()


def hand_over(*refs):
    count = len(refs) // 2
    for k in range(count):
        refs[count + k][...] = refs[k][...]


def local(
    n,
    n_dom,
    tire_pos,
    tire_vel,
    part_pos,
    part_vel,
    contact_owner,
    contact_tile,
    halo_tiles,
    block_inverse,
    pattern,
    coupling,
):
    nb = tire_pos.shape[1] // BLK
    nt = part_pos.shape[1] // BLK
    vmem = pl.BlockSpec(memory_space=pltpu.VMEM)
    hbm = pl.BlockSpec(memory_space=pltpu.HBM)
    message = pltpu.VMEM((n * 8, BLK), F32)
    outs = (
        jax.ShapeDtypeStruct(tire_pos.shape, F32),
        jax.ShapeDtypeStruct(tire_pos.shape, F32),
        jax.ShapeDtypeStruct(part_pos.shape, F32),
        jax.ShapeDtypeStruct(part_pos.shape, F32),
    )
    results = pl.pallas_call(
        functools.partial(kernel, n, n_dom, nb, nt),
        out_shape=outs,
        in_specs=[hbm] * 10,
        out_specs=[vmem] * 4,
        scratch_shapes=[
            pltpu.VMEM(tire_pos.shape, F32),
            pltpu.VMEM(tire_pos.shape, F32),
            pltpu.VMEM(part_pos.shape, F32),
            pltpu.VMEM(part_pos.shape, F32),
            pltpu.VMEM((TOPC, nb), jnp.int32),
            pltpu.VMEM((TOPC, nb), jnp.int32),
            pltpu.SMEM((HB,), jnp.int32),
            pltpu.VMEM((NNZB, nb), jnp.int32),
            pltpu.VMEM((NNZB, nb), F32),
            pltpu.VMEM((GROUP, 2 * BLK, 2 * BLK), BF),
            pltpu.VMEM((nb, BLK, BLK), F32),
            pltpu.VMEM((nb // 2, 2 * BLK, 2 * BLK), BF),
            pltpu.VMEM((nb * 8, BLK), F32),
            pltpu.VMEM((nt * 8, BLK), F32),
        ]
        + [message] * 12
        + [
            pltpu.VMEM((32, BLK), F32),
            pltpu.VMEM((32, BLK), F32),
            pltpu.VMEM((16, BLK), F32),
            pltpu.VMEM((nb * 8, BLK), F32),
            pltpu.VMEM((nb * 8, BLK), F32),
            pltpu.VMEM((3, 2 * nt, 3 * BLK), BF),
            pltpu.VMEM((2, BLK, BLK), BF),
            pltpu.VMEM((2, BLK, BLK), BF),
            pltpu.VMEM((2, BLK, BLK), BF),
            pltpu.VMEM((BLK, BLK), BF),
            pltpu.SemaphoreType.DMA((9,)),
            pltpu.SemaphoreType.DMA,
            pltpu.SemaphoreType.DMA((4,)),
            pltpu.SemaphoreType.DMA((n // GROUP,)),
            pltpu.SemaphoreType.DMA,
            pltpu.SemaphoreType.DMA((n // GROUP,)),
            pltpu.SemaphoreType.DMA,
            pltpu.SemaphoreType.DMA((2,)),
            pltpu.SemaphoreType.DMA((2,)),
        ],
        compiler_params=pltpu.CompilerParams(
            collective_id=0, has_side_effects=True, vmem_limit_bytes=62 << 20
        ),
    )(
        tire_pos,
        tire_vel,
        part_pos,
        part_vel,
        contact_owner.T,
        contact_tile.T,
        halo_tiles,
        block_inverse,
        pattern.T,
        coupling.T,
    )
    return pl.pallas_call(
        hand_over,
        out_shape=outs,
        in_specs=[vmem] * 4,
        out_specs=[vmem] * 4,
        compiler_params=pltpu.CompilerParams(vmem_limit_bytes=62 << 20),
    )(*results)


def solution(mesh):
    n_role, n_dom = mesh.shape["role"], mesh.shape["dom"]
    both = ("role", "dom")
    return jax.shard_map(
        functools.partial(local, n_role * n_dom, n_dom),
        mesh=mesh,
        in_specs=(
            P(None, both),
            P(None, both),
            P(None, both),
            P(None, both),
            P(both, None),
            P(both, None),
            P(both),
            P(both, None, None),
            P(both, None),
            P(both, None),
        ),
        out_specs=(P(None, both), P(None, both), P(None, both), P(None, both)),
        check_vma=False,
    )
```

```python
import functools
import math

import jax
import jax.numpy as jnp
from jax import lax
from jax.experimental import pallas as pl
from jax.experimental.pallas import tpu as pltpu
from jax.sharding import PartitionSpec as P

BLK = 128
TOPC = 2
NNZB = 3
SWEEPS = 3
HB = 4
GROUP = 16

BF = jnp.bfloat16
F32 = jnp.float32
MESH = pl.DeviceIdType.MESH

gain = 0.05
time_step = 0.1
spread_sq = 4.0
SCALE = math.sqrt(2.0 * math.log2(math.e) / spread_sq)


def split2(x):
    hi = x.astype(BF).astype(F32)
    return hi, x - hi


def split3(x):
    hi = x.astype(BF).astype(F32)
    rest = x - hi
    mid = rest.astype(BF).astype(F32)
    return hi, mid, rest - mid


def dot(a, b):
    return jnp.dot(a, b, preferred_element_type=F32)


def dot_nt(a, b):
    return lax.dot_general(a, b, (((1,), (1,)), ((), ())), preferred_element_type=F32)


def dot_tn(a, b):
    return lax.dot_general(a, b, (((0,), (0,)), ((), ())), preferred_element_type=F32)


def pair_weights(near, far):
    row = lax.broadcasted_iota(jnp.int32, (8, BLK), 0)
    near_s = near * SCALE
    far_s = far * SCALE

    def norms(t):
        sq = t * t * (-0.5)
        first = jnp.sum(jnp.where(row < 3, sq, 0.0), axis=0, keepdims=True)
        second = jnp.sum(
            jnp.where((row >= 3) & (row < 6), sq, 0.0), axis=0, keepdims=True
        )
        return first, second

    nx0, nx1 = norms(near_s)
    ny = norms(far_s)
    xh, xm, xl = split3(jnp.where(row < 6, near_s, jnp.where(row == 6, nx0, nx1)))
    one = jnp.ones((8, BLK), F32)
    lhs = jnp.concatenate([xh, xm, xl, xh, xm, xh, one, one], axis=0).astype(BF)
    yh, ym, yl = split3(jnp.where(row < 6, far_s, 0.0))
    sides = []
    for k in range(2):
        mask = (row >= 3 * k) & (row < 3 * k + 3)

        def keep(t):
            return jnp.where(mask, t, 0.0)

        yhk = keep(yh) + (row == 6 + k).astype(F32)
        nh, nm, nl = split3(ny[k])
        nrows = jnp.where(
            row == 0, nh, jnp.where(row == 1, nm, jnp.where(row == 2, nl, 0.0))
        )
        sides.append(
            jnp.concatenate(
                [yhk, yhk, yhk, keep(ym), keep(ym), keep(yl), nrows, one * 0.0], axis=0
            )
        )
    rhs = jnp.concatenate(sides, axis=1).astype(BF)
    weight = jnp.exp2(jnp.minimum(dot_tn(lhs, rhs), 0.0))
    w_hi = weight.astype(BF)
    return w_hi, (weight - w_hi.astype(F32)).astype(BF)


def features(t):
    row = lax.broadcasted_iota(jnp.int32, (8, BLK), 0)
    h, l = split2(t)
    h = jnp.where(row == 6, 1.0, jnp.where(row == 7, 0.0, h))
    l = jnp.where(row < 6, l, 0.0)
    return jnp.concatenate([h, l], axis=0).astype(BF)


def force(t, a, b):
    row = lax.broadcasted_iota(jnp.int32, (8, BLK), 0)
    a = a[0:8] + a[8:16]
    b = b[0:8] + b[8:16]
    total = jnp.where(row < 3, a[6:7, :], b[6:7, :])
    return gain * (t * total - jnp.where(row < 3, a, b))


def put_weights(ws, u, near, far):
    ws[u, 0:BLK, :], ws[u, BLK : 2 * BLK, :] = pair_weights(near, far)


def react_of(ws, u, near, far):
    f = features(near)
    o = dot(jnp.concatenate([f, f], axis=1), ws[u])
    return force(far, o[:, :BLK], o[:, BLK:])


def push_of(ws, u, near, far):
    f = features(far)
    a = dot_nt(f, ws[u, :, :BLK])
    b = dot_nt(f, ws[u, :, BLK:])
    return force(near, a[:, :BLK] + a[:, BLK:], b[:, :BLK] + b[:, BLK:])


def kernel(
    n,
    n_dom,
    nb,
    nt,
    tire_pos,
    tire_vel,
    part_pos,
    part_vel,
    owner,
    ctile,
    halo,
    binv,
    pattern,
    coup,
    o_tp,
    o_tv,
    o_pp,
    o_pv,
    s_tp,
    s_tv,
    s_pp,
    s_pv,
    s_owner,
    s_ctile,
    s_halo,
    s_pattern,
    s_coup,
    ws,
    bstage,
    bsplit,
    nscr,
    pscr,
    send1,
    near1,
    far1,
    push1,
    pret,
    react1,
    tsend,
    tret,
    near2,
    push2,
    react2,
    rret,
    edge,
    hrecv,
    hpush,
    vs,
    vo,
    tst,
    sk_t,
    sk_n,
    oh_n,
    oh_t,
    insem,
    bsem,
    ssem,
    rsem1,
    psem,
    tsem,
    rrsem,
    hsem,
    hssem,
):
    me = lax.axis_index("role") * n_dom + lax.axis_index("dom")

    def dev(p):
        return (p // n_dom, p % n_dom)

    def ahead(i):
        return dev((me + i) % n)

    def behind(i):
        return dev((me + n - i) % n)

    arrive = []
    for k, (src, dst) in enumerate(
        [
            (tire_pos, s_tp),
            (owner, s_owner),
            (ctile, s_ctile),
            (part_pos, s_pp),
            (halo, s_halo),
            (part_vel, s_pv),
            (tire_vel, s_tv),
            (pattern, s_pattern),
            (coup, s_coup),
        ]
    ):
        arrive.append(pltpu.make_async_copy(src, dst, insem.at[k]))
        arrive[k].start()

    def ready(first, last):
        for k in range(first, last):
            arrive[k].wait()

    barrier = pltpu.get_barrier_semaphore()

    def greet(i, c):
        pl.semaphore_signal(barrier, inc=1, device_id=ahead(i), device_id_type=MESH)
        return c

    lax.fori_loop(1, n, greet, 0)

    bcopy = pltpu.make_async_copy(binv, bstage, bsem)
    bcopy.start()

    def tile_rows(i, rows=8):
        return pl.ds(pl.multiple_of(i * 8, 8), rows)

    def comps(ref, count, first=0):
        return [ref[pl.ds(first + c, count, stride=8), :] for c in range(3)]

    def put(ref, count, vals, first=0):
        for c in range(len(vals)):
            ref[pl.ds(first + c, count, stride=8), :] = vals[c]

    def spread(src, scr, count):
        for b in range(count):
            scr[b * 8 : b * 8 + 3, :] = src[:, b * BLK : (b + 1) * BLK]

    def collect(scr, dst, count):
        for b in range(count):
            dst[:, b * BLK : (b + 1) * BLK] = scr[b * 8 : b * 8 + 3, :]

    lane = lax.broadcasted_iota(jnp.int32, (BLK, BLK), 1)
    sub = lax.broadcasted_iota(jnp.int32, (BLK, BLK), 0)

    def pad_rows(x, rows=BLK):
        if x.shape[0] == rows:
            return x
        return jnp.concatenate(
            [x, jnp.zeros((rows - x.shape[0], x.shape[1]), x.dtype)], axis=0
        )

    ready(0, 3)
    sub_b = lax.broadcasted_iota(jnp.int32, (BLK, nb), 0)
    hot = jnp.zeros((BLK, nb), F32)
    tile_of = jnp.zeros((BLK, nb), F32)
    for m in range(TOPC):
        rel = (s_owner[m : m + 1, :] - me + n) & (n - 1)
        is_m = sub_b == rel
        hot = hot + jnp.where(is_m, 1.0, 0.0)
        tile_of = tile_of + jnp.where(
            is_m, (s_ctile[m : m + 1, :] + 1).astype(F32), 0.0
        )

    def pad_lanes(x):
        return jnp.concatenate([x, jnp.zeros((BLK, BLK - nb), x.dtype)], axis=1)

    hot_p = pad_lanes(hot)
    upper = jnp.where(sub < lane, 1.0, 0.0).astype(BF)
    rank = dot(hot_p.astype(BF), upper)
    tile_p = pad_lanes(tile_of)
    ids = []
    for k in range(2):
        u = jnp.where((hot_p > 0.5) & (jnp.abs(rank - k) < 0.5), tile_p, 0.0)
        sk_n[k] = jnp.where(u > 0.5, 1.0, 0.0).astype(BF)
        ids.append(jnp.sum(u, axis=1, keepdims=True) - 1.0)

    def node_slots(x, dst):
        cat = jnp.concatenate(x, axis=1)
        parts = [pad_rows(t.astype(BF)) for t in split3(cat)]
        for k in range(2):
            g = dot(sk_n[k], parts[0]) + dot(sk_n[k], parts[1]) + dot(sk_n[k], parts[2])
            put(dst, n, [g[:, c * BLK : (c + 1) * BLK] for c in range(3)], 3 * k)

    spread(s_tp, nscr, nb)
    tp = comps(nscr, nb)
    node_slots(tp, send1)
    send1[pl.ds(6, n, stride=8), :] = jnp.where(
        lane < nt, jnp.broadcast_to(ids[0], (n, BLK)), jnp.broadcast_to(ids[1], (n, BLK))
    )

    pl.semaphore_wait(barrier, n - 1)

    def wait_rows(ref, sem, count, rows):
        view = ref.at[pl.ds(0, count * rows), :]
        pltpu.make_async_copy(view, view, sem).wait()

    def remote(src, dst, i, rows, sem_s, sem_r, target):
        pltpu.make_async_remote_copy(
            src_ref=src.at[tile_rows(i, rows), :],
            dst_ref=dst.at[tile_rows(i, rows), :],
            send_sem=sem_s,
            recv_sem=sem_r,
            device_id=target,
            device_id_type=MESH,
        ).start()

    def own(src, dst, rows, sem_r):
        pltpu.make_async_copy(
            src.at[pl.ds(0, rows), :], dst.at[pl.ds(0, rows), :], sem_r
        ).start()

    own(send1, near1, 7, rsem1.at[0])

    def send_pos(i, c):
        remote(send1, near1, i, 7, ssem.at[0], rsem1.at[i // GROUP], ahead(i))
        return c

    lax.fori_loop(1, n, send_pos, 0)

    def tiles_split(x):
        cat = jnp.concatenate(x, axis=1)
        for s, t in enumerate(split3(cat)):
            t = t.astype(BF)
            tst[s, 0:nt, :] = t
            tst[s, nt : 2 * nt, :] = t

    def send_edges(step):
        for u in range(2):
            a = pscr[pl.ds(s_halo[2 * u] * 8, 8), :]
            b = pscr[pl.ds(s_halo[2 * u + 1] * 8, 8), :]
            edge[pl.ds((2 * step + u) * 8, 8), :] = jnp.concatenate(
                [a[0:3], b[0:3], jnp.zeros((2, BLK), F32)], axis=0
            )
        pltpu.make_async_remote_copy(
            src_ref=edge.at[pl.ds(step * 16, 16), :],
            dst_ref=hrecv.at[pl.ds(step * 16, 16), :],
            send_sem=hssem.at[step],
            recv_sem=hsem.at[step],
            device_id=ahead(1),
            device_id_type=MESH,
        ).start()

    ready(3, 5)
    spread(s_pp, pscr, nt)
    pp = comps(pscr, nt)
    tiles_split(pp)
    send_edges(0)

    live = jnp.where(me > 0, 1.0, 0.0).astype(F32)
    sub_t = lax.broadcasted_iota(jnp.int32, (nt, BLK), 0)

    def halo_force(step):
        view = hrecv.at[pl.ds(step * 16, 16), :]
        pltpu.make_async_copy(view, view, hsem.at[step]).wait()
        out = [jnp.zeros((nt, BLK), F32) for _ in range(3)]
        for u in range(2):
            at = pl.ds((2 * step + u) * 8, 8)
            put_weights(ws, u, edge[at, :], hrecv[at, :])
            push = push_of(ws, u, edge[at, :], hrecv[at, :]) * live
            for k in range(2):
                here = sub_t == s_halo[2 * u + k]
                for c in range(3):
                    r = 3 * k + c
                    out[c] = out[c] + jnp.where(here, push[r : r + 1, :], 0.0)
        return out

    for k in range(2):
        sk_t[k] = jnp.transpose(sk_n[k].astype(F32)).astype(BF)
    ready(5, 9)
    bcopy.wait()

    def split_block(q, c):
        for s in range(2):
            b = jnp.transpose(bstage[2 * q + s])
            hi = b.astype(BF)
            bsplit[q, 0:BLK, s * BLK : (s + 1) * BLK] = hi
            bsplit[q, BLK : 2 * BLK, s * BLK : (s + 1) * BLK] = (
                b - hi.astype(F32)
            ).astype(BF)
        return c

    lax.fori_loop(0, nb // 2, split_block, 0, unroll=4)

    cmat = jnp.zeros((BLK, nb), F32)
    for m in range(NNZB):
        cmat = cmat + jnp.where(
            sub_b == s_pattern[m : m + 1, :], s_coup[m : m + 1, :], 0.0
        )
    cmat = jnp.transpose(pad_lanes(cmat))[0:nb]
    c_hi = cmat.astype(BF)
    c_lo = (cmat - c_hi.astype(F32)).astype(BF)
    vs[...] = jnp.zeros_like(vs)

    def matvec(x):
        for c in range(3):
            h, l = split2(x[c])
            vs[pl.ds(c, nb, stride=8), :] = h
            vs[pl.ds(3 + c, nb, stride=8), :] = l

        for q in range(nb // 2):
            at = pl.ds(q * 16, 16)
            t = vs[at, :].astype(BF)
            o = dot(jnp.concatenate([t, t], axis=1), bsplit[q])
            vo[at, :] = jnp.concatenate([o[0:8, :BLK], o[8:16, BLK:]], axis=0)
        a, b = comps(vo, nb), comps(vo, nb, 3)
        return [a[c] + b[c] for c in range(3)]

    def couple(v):
        h, l = split2(jnp.concatenate(v, axis=1))
        h, l = pad_rows(h.astype(BF)), pad_rows(l.astype(BF))
        o = dot(c_hi, h) + dot(c_lo, h) + dot(c_hi, l)
        return [o[:, c * BLK : (c + 1) * BLK] for c in range(3)]

    def solve(rhs):
        v = matvec(rhs)
        for _ in range(SWEEPS):
            w = couple(v)
            v = matvec([rhs[c] + w[c] for c in range(3)])
        return v

    def by_slot(ref, k):
        return jnp.concatenate(comps(ref, n, 3 * k), axis=1)

    def gather_sum(mats, ref):
        total = None
        for k in range(2):
            h, l = split2(by_slot(ref, k))
            o = dot(mats[k], h.astype(BF)) + dot(mats[k], l.astype(BF))
            total = o if total is None else total + o
        return [total[:, c * BLK : (c + 1) * BLK] for c in range(3)]

    def soil_sum(ref):
        return gather_sum([oh_t[0:nt, :], oh_t[nt : 2 * nt, :]], ref)

    def node_sum(ref):
        return gather_sum([sk_t[0, 0:nb, :], sk_t[1, 0:nb, :]], ref)

    lane_g = lax.broadcasted_iota(jnp.int32, (GROUP, BLK), 1)
    lane_gm = (lane_g & (nt - 1)).astype(F32)

    def pairs(g, near, far, push, react):
        for u in range(GROUP):
            at = tile_rows(g * GROUP + u)
            put_weights(ws, u, near[at, :], far[at, :])
        for u in range(GROUP):
            at = tile_rows(g * GROUP + u)
            react[at, :] = react_of(ws, u, near[at, :], far[at, :])
            push[at, :] = push_of(ws, u, near[at, :], far[at, :])

    def owner_group(g, c):
        base = pl.multiple_of(g * GROUP * 8, GROUP * 8)
        wait_rows(near1, rsem1.at[g], GROUP, 7)
        tid = near1[pl.ds(base + 6, GROUP, stride=8), :]
        oh = jnp.where(tid == lane_gm, 1.0, 0.0)
        sel = jnp.concatenate(
            [jnp.where(lane_g < nt, oh, 0.0), jnp.where(lane_g < nt, 0.0, oh)], axis=0
        ).astype(BF)
        got = dot(sel, tst[0]) + dot(sel, tst[1]) + dot(sel, tst[2])
        for k in range(2):
            for cc in range(3):
                far1[pl.ds(base + 3 * k + cc, GROUP, stride=8), :] = got[
                    k * GROUP : (k + 1) * GROUP, cc * BLK : (cc + 1) * BLK
                ]

        pairs(g, near1, far1, push1, react1)
        for u in range(GROUP):
            i = g * GROUP + u
            if u > 0:
                remote(push1, pret, i, 6, ssem.at[1], psem, behind(i))
            else:

                @pl.when(i > 0)
                def _():
                    remote(push1, pret, i, 6, ssem.at[1], psem, behind(i))

                @pl.when(i == 0)
                def _():
                    own(push1, pret, 6, psem)

        return c

    lax.fori_loop(0, n // GROUP, owner_group, 0)

    lane_m = (lane & (nt - 1)).astype(F32)
    oh_all = jnp.where(near1[pl.ds(6, n, stride=8), :] == lane_m, 1.0, 0.0)
    oh_n[0] = jnp.where(lane < nt, oh_all, 0.0).astype(BF)
    oh_n[1] = jnp.where(lane < nt, 0.0, oh_all).astype(BF)
    oh_t[...] = jnp.transpose(oh_all).astype(BF)

    hf = halo_force(0)
    sf = soil_sum(react1)
    spread(s_pv, pscr, nt)
    pv = comps(pscr, nt)
    pv = [pv[c] + time_step * (sf[c] + hf[c]) for c in range(3)]
    pp = [pp[c] + time_step * pv[c] for c in range(3)]
    put(pscr, nt, pp)
    tiles_split(pp)
    for k in range(2):
        got = dot(oh_n[k], tst[0]) + dot(oh_n[k], tst[1]) + dot(oh_n[k], tst[2])
        put(tsend, n, [got[:, c * BLK : (c + 1) * BLK] for c in range(3)], 3 * k)

    own(tsend, tret, 6, tsem.at[0])

    def send_tiles(i, c):
        remote(tsend, tret, i, 6, ssem.at[2], tsem.at[i // GROUP], behind(i))
        return c

    lax.fori_loop(1, n, send_tiles, 0)
    send_edges(1)

    spread(s_tv, nscr, nb)
    tv = comps(nscr, nb)
    wait_rows(pret, psem, n, 6)
    nf = node_sum(pret)
    tv = solve([tv[c] + time_step * nf[c] for c in range(3)])
    tp = [tp[c] + time_step * tv[c] for c in range(3)]
    node_slots(tp, near2)

    def node_group(g, c):
        wait_rows(tret, tsem.at[g], GROUP, 6)

        pairs(g, near2, tret, push2, react2)
        for u in range(GROUP):
            i = g * GROUP + u
            if u > 0:
                remote(react2, rret, i, 6, ssem.at[3], rrsem, ahead(i))
            else:

                @pl.when(i > 0)
                def _():
                    remote(react2, rret, i, 6, ssem.at[3], rrsem, ahead(i))

                @pl.when(i == 0)
                def _():
                    own(react2, rret, 6, rrsem)

        return c

    lax.fori_loop(0, n // GROUP, node_group, 0)

    nf = node_sum(push2)
    tv = solve([tv[c] + time_step * nf[c] for c in range(3)])
    tp = [tp[c] + time_step * tv[c] for c in range(3)]
    put(nscr, nb, tv)
    collect(nscr, o_tv, nb)
    put(nscr, nb, tp)
    collect(nscr, o_tp, nb)

    hf = halo_force(1)
    wait_rows(rret, rrsem, n, 6)
    sf = soil_sum(rret)
    pv = [pv[c] + time_step * (sf[c] + hf[c]) for c in range(3)]
    pp = [pp[c] + time_step * pv[c] for c in range(3)]
    put(pscr, nt, pv)
    collect(pscr, o_pv, nt)
    put(pscr, nt, pp)
    collect(pscr, o_pp, nt)

    wait_rows(send1, ssem.at[0], n - 1, 7)
    for s in range(1, 4):
        wait_rows(push1, ssem.at[s], n - 1, 6)
    for step in range(2):
        view = edge.at[pl.ds(step * 16, 16), :]
        pltpu.make_async_copy(view, view, hssem.at[step]).wait()


def hand_over(*refs):
    count = len(refs) // 2
    for k in range(count):
        refs[count + k][...] = refs[k][...]


def local(
    n,
    n_dom,
    tire_pos,
    tire_vel,
    part_pos,
    part_vel,
    contact_owner,
    contact_tile,
    halo_tiles,
    block_inverse,
    pattern,
    coupling,
):
    nb = tire_pos.shape[1] // BLK
    nt = part_pos.shape[1] // BLK
    vmem = pl.BlockSpec(memory_space=pltpu.VMEM)
    hbm = pl.BlockSpec(memory_space=pltpu.HBM)
    message = pltpu.VMEM((n * 8, BLK), F32)
    outs = (
        jax.ShapeDtypeStruct(tire_pos.shape, F32),
        jax.ShapeDtypeStruct(tire_pos.shape, F32),
        jax.ShapeDtypeStruct(part_pos.shape, F32),
        jax.ShapeDtypeStruct(part_pos.shape, F32),
    )
    results = pl.pallas_call(
        functools.partial(kernel, n, n_dom, nb, nt),
        out_shape=outs,
        in_specs=[hbm] * 10,
        out_specs=[vmem] * 4,
        scratch_shapes=[
            pltpu.VMEM(tire_pos.shape, F32),
            pltpu.VMEM(tire_pos.shape, F32),
            pltpu.VMEM(part_pos.shape, F32),
            pltpu.VMEM(part_pos.shape, F32),
            pltpu.VMEM((TOPC, nb), jnp.int32),
            pltpu.VMEM((TOPC, nb), jnp.int32),
            pltpu.SMEM((HB,), jnp.int32),
            pltpu.VMEM((NNZB, nb), jnp.int32),
            pltpu.VMEM((NNZB, nb), F32),
            pltpu.VMEM((GROUP, 2 * BLK, 2 * BLK), BF),
            pltpu.VMEM((nb, BLK, BLK), F32),
            pltpu.VMEM((nb // 2, 2 * BLK, 2 * BLK), BF),
            pltpu.VMEM((nb * 8, BLK), F32),
            pltpu.VMEM((nt * 8, BLK), F32),
        ]
        + [message] * 12
        + [
            pltpu.VMEM((32, BLK), F32),
            pltpu.VMEM((32, BLK), F32),
            pltpu.VMEM((16, BLK), F32),
            pltpu.VMEM((nb * 8, BLK), F32),
            pltpu.VMEM((nb * 8, BLK), F32),
            pltpu.VMEM((3, 2 * nt, 3 * BLK), BF),
            pltpu.VMEM((2, BLK, BLK), BF),
            pltpu.VMEM((2, BLK, BLK), BF),
            pltpu.VMEM((2, BLK, BLK), BF),
            pltpu.VMEM((BLK, BLK), BF),
            pltpu.SemaphoreType.DMA((9,)),
            pltpu.SemaphoreType.DMA,
            pltpu.SemaphoreType.DMA((4,)),
            pltpu.SemaphoreType.DMA((n // GROUP,)),
            pltpu.SemaphoreType.DMA,
            pltpu.SemaphoreType.DMA((n // GROUP,)),
            pltpu.SemaphoreType.DMA,
            pltpu.SemaphoreType.DMA((2,)),
            pltpu.SemaphoreType.DMA((2,)),
        ],
        compiler_params=pltpu.CompilerParams(
            collective_id=0, has_side_effects=True, vmem_limit_bytes=62 << 20
        ),
    )(
        tire_pos,
        tire_vel,
        part_pos,
        part_vel,
        contact_owner.T,
        contact_tile.T,
        halo_tiles,
        block_inverse,
        pattern.T,
        coupling.T,
    )
    return pl.pallas_call(
        hand_over,
        out_shape=outs,
        in_specs=[vmem] * 4,
        out_specs=[vmem] * 4,
        compiler_params=pltpu.CompilerParams(vmem_limit_bytes=62 << 20),
    )(*results)


def solution(mesh):
    n_role, n_dom = mesh.shape["role"], mesh.shape["dom"]
    both = ("role", "dom")
    return jax.shard_map(
        functools.partial(local, n_role * n_dom, n_dom),
        mesh=mesh,
        in_specs=(
            P(None, both),
            P(None, both),
            P(None, both),
            P(None, both),
            P(both, None),
            P(both, None),
            P(both),
            P(both, None, None),
            P(both, None),
            P(both, None),
        ),
        out_specs=(P(None, both), P(None, both), P(None, both), P(None, both)),
        check_vma=False,
    )
```

```python
import functools
import math

import jax
import jax.numpy as jnp
from jax import lax
from jax.experimental import pallas as pl
from jax.experimental.pallas import tpu as pltpu
from jax.sharding import PartitionSpec as P

BLK = 128
TOPC = 2
NNZB = 3
SWEEPS = 3
HB = 4
GROUP = 16

BF = jnp.bfloat16
F32 = jnp.float32
MESH = pl.DeviceIdType.MESH

gain = 0.05
time_step = 0.1
spread_sq = 4.0
SCALE = math.sqrt(2.0 * math.log2(math.e) / spread_sq)


def split2(x):
    hi = x.astype(BF).astype(F32)
    return hi, x - hi


def split3(x):
    hi = x.astype(BF).astype(F32)
    rest = x - hi
    mid = rest.astype(BF).astype(F32)
    return hi, mid, rest - mid


def dot(a, b):
    return jnp.dot(a, b, preferred_element_type=F32)


def dot_nt(a, b):
    return lax.dot_general(a, b, (((1,), (1,)), ((), ())), preferred_element_type=F32)


def dot_tn(a, b):
    return lax.dot_general(a, b, (((0,), (0,)), ((), ())), preferred_element_type=F32)


def pair_weights(near, far):
    row = lax.broadcasted_iota(jnp.int32, (8, BLK), 0)
    near_s = near * SCALE
    far_s = far * SCALE

    def norms(t):
        sq = t * t * (-0.5)
        first = jnp.sum(jnp.where(row < 3, sq, 0.0), axis=0, keepdims=True)
        second = jnp.sum(
            jnp.where((row >= 3) & (row < 6), sq, 0.0), axis=0, keepdims=True
        )
        return first, second

    nx0, nx1 = norms(near_s)
    ny = norms(far_s)
    xh, xm, xl = split3(jnp.where(row < 6, near_s, jnp.where(row == 6, nx0, nx1)))
    one = jnp.ones((8, BLK), F32)
    lhs = jnp.concatenate([xh, xm, xl, xh, xm, xh, one, one], axis=0).astype(BF)
    yh, ym, yl = split3(jnp.where(row < 6, far_s, 0.0))
    sides = []
    for k in range(2):
        mask = (row >= 3 * k) & (row < 3 * k + 3)

        def keep(t):
            return jnp.where(mask, t, 0.0)

        yhk = keep(yh) + (row == 6 + k).astype(F32)
        nh, nm, nl = split3(ny[k])
        nrows = jnp.where(
            row == 0, nh, jnp.where(row == 1, nm, jnp.where(row == 2, nl, 0.0))
        )
        sides.append(
            jnp.concatenate(
                [yhk, yhk, yhk, keep(ym), keep(ym), keep(yl), nrows, one * 0.0], axis=0
            )
        )
    rhs = jnp.concatenate(sides, axis=1).astype(BF)
    weight = jnp.exp2(jnp.minimum(dot_tn(lhs, rhs), 0.0))
    w_hi = weight.astype(BF)
    return w_hi, (weight - w_hi.astype(F32)).astype(BF)


def features(t):
    row = lax.broadcasted_iota(jnp.int32, (8, BLK), 0)
    h, l = split2(t)
    h = jnp.where(row == 6, 1.0, jnp.where(row == 7, 0.0, h))
    l = jnp.where(row < 6, l, 0.0)
    return jnp.concatenate([h, l], axis=0).astype(BF)


def force(t, a, b):
    row = lax.broadcasted_iota(jnp.int32, (8, BLK), 0)
    a = a[0:8] + a[8:16]
    b = b[0:8] + b[8:16]
    total = jnp.where(row < 3, a[6:7, :], b[6:7, :])
    return gain * (t * total - jnp.where(row < 3, a, b))


def put_weights(ws, u, near, far):
    ws[u, 0:BLK, :], ws[u, BLK : 2 * BLK, :] = pair_weights(near, far)


def react_of(ws, u, near, far):
    f = features(near)
    o = dot(jnp.concatenate([f, f], axis=1), ws[u])
    return force(far, o[:, :BLK], o[:, BLK:])


def push_of(ws, u, near, far):
    f = features(far)
    a = dot_nt(f, ws[u, :, :BLK])
    b = dot_nt(f, ws[u, :, BLK:])
    return force(near, a[:, :BLK] + a[:, BLK:], b[:, :BLK] + b[:, BLK:])


def kernel(
    n,
    n_dom,
    nb,
    nt,
    tire_pos,
    tire_vel,
    part_pos,
    part_vel,
    owner,
    ctile,
    halo,
    binv,
    pattern,
    coup,
    o_tp,
    o_tv,
    o_pp,
    o_pv,
    s_tp,
    s_tv,
    s_pp,
    s_pv,
    s_owner,
    s_ctile,
    s_halo,
    s_pattern,
    s_coup,
    ws,
    bstage,
    bsplit,
    nscr,
    pscr,
    send1,
    near1,
    far1,
    push1,
    pret,
    react1,
    tsend,
    tret,
    near2,
    push2,
    react2,
    rret,
    edge,
    hrecv,
    hpush,
    vs,
    vo,
    tst,
    sk_t,
    sk_n,
    oh_n,
    oh_t,
    insem,
    bsem,
    ssem,
    rsem1,
    psem,
    tsem,
    rrsem,
    hsem,
    hssem,
):
    me = lax.axis_index("role") * n_dom + lax.axis_index("dom")

    def dev(p):
        return (lax.div(p, n_dom), lax.rem(p, n_dom))

    def ahead(i):
        return dev(lax.rem(me + i, n))

    def behind(i):
        return dev(lax.rem(me + n - i, n))

    arrive = []
    for k, (src, dst) in enumerate(
        [
            (tire_pos, s_tp),
            (owner, s_owner),
            (ctile, s_ctile),
            (part_pos, s_pp),
            (halo, s_halo),
            (part_vel, s_pv),
            (tire_vel, s_tv),
            (pattern, s_pattern),
            (coup, s_coup),
        ]
    ):
        arrive.append(pltpu.make_async_copy(src, dst, insem.at[k]))
        arrive[k].start()

    def ready(first, last):
        for k in range(first, last):
            arrive[k].wait()

    barrier = pltpu.get_barrier_semaphore()

    def greet(i, c):
        pl.semaphore_signal(barrier, inc=1, device_id=ahead(i), device_id_type=MESH)
        return c

    lax.fori_loop(1, n, greet, 0)

    bcopy = pltpu.make_async_copy(binv, bstage, bsem)
    bcopy.start()

    def tile_rows(i, rows=8):
        return pl.ds(pl.multiple_of(i * 8, 8), rows)

    def comps(ref, count, first=0):
        return [ref[pl.ds(first + c, count, stride=8), :] for c in range(3)]

    def put(ref, count, vals, first=0):
        for c in range(len(vals)):
            ref[pl.ds(first + c, count, stride=8), :] = vals[c]

    def spread(src, scr, count):
        for b in range(count):
            scr[b * 8 : b * 8 + 3, :] = src[:, b * BLK : (b + 1) * BLK]

    def collect(scr, dst, count):
        for b in range(count):
            dst[:, b * BLK : (b + 1) * BLK] = scr[b * 8 : b * 8 + 3, :]

    lane = lax.broadcasted_iota(jnp.int32, (BLK, BLK), 1)
    sub = lax.broadcasted_iota(jnp.int32, (BLK, BLK), 0)

    def pad_rows(x, rows=BLK):
        if x.shape[0] == rows:
            return x
        return jnp.concatenate(
            [x, jnp.zeros((rows - x.shape[0], x.shape[1]), x.dtype)], axis=0
        )

    ready(0, 3)
    sub_b = lax.broadcasted_iota(jnp.int32, (BLK, nb), 0)
    hot = jnp.zeros((BLK, nb), F32)
    tile_of = jnp.zeros((BLK, nb), F32)
    for m in range(TOPC):
        rel = (s_owner[m : m + 1, :] - me + n) & (n - 1)
        is_m = sub_b == rel
        hot = hot + jnp.where(is_m, 1.0, 0.0)
        tile_of = tile_of + jnp.where(
            is_m, (s_ctile[m : m + 1, :] + 1).astype(F32), 0.0
        )

    def pad_lanes(x):
        return jnp.concatenate([x, jnp.zeros((BLK, BLK - nb), x.dtype)], axis=1)

    hot_p = pad_lanes(hot)
    upper = jnp.where(sub < lane, 1.0, 0.0).astype(BF)
    rank = dot(hot_p.astype(BF), upper)
    tile_p = pad_lanes(tile_of)
    ids = []
    for k in range(2):
        u = jnp.where((hot_p > 0.5) & (jnp.abs(rank - k) < 0.5), tile_p, 0.0)
        sk_n[k] = jnp.where(u > 0.5, 1.0, 0.0).astype(BF)
        ids.append(jnp.sum(u, axis=1, keepdims=True) - 1.0)

    def node_slots(x, dst):
        cat = jnp.concatenate(x, axis=1)
        parts = [pad_rows(t.astype(BF)) for t in split3(cat)]
        for k in range(2):
            g = dot(sk_n[k], parts[0]) + dot(sk_n[k], parts[1]) + dot(sk_n[k], parts[2])
            put(dst, n, [g[:, c * BLK : (c + 1) * BLK] for c in range(3)], 3 * k)

    spread(s_tp, nscr, nb)
    tp = comps(nscr, nb)
    node_slots(tp, send1)
    send1[pl.ds(6, n, stride=8), :] = jnp.where(
        lane < nt, jnp.broadcast_to(ids[0], (n, BLK)), jnp.broadcast_to(ids[1], (n, BLK))
    )

    pl.semaphore_wait(barrier, n - 1)

    def wait_rows(ref, sem, count, rows):
        view = ref.at[pl.ds(0, count * rows), :]
        pltpu.make_async_copy(view, view, sem).wait()

    def remote(src, dst, i, rows, sem_s, sem_r, target):
        pltpu.make_async_remote_copy(
            src_ref=src.at[tile_rows(i, rows), :],
            dst_ref=dst.at[tile_rows(i, rows), :],
            send_sem=sem_s,
            recv_sem=sem_r,
            device_id=target,
            device_id_type=MESH,
        ).start()

    def own(src, dst, rows, sem_r):
        pltpu.make_async_copy(
            src.at[pl.ds(0, rows), :], dst.at[pl.ds(0, rows), :], sem_r
        ).start()

    own(send1, near1, 7, rsem1.at[0])

    def send_pos(i, c):
        remote(send1, near1, i, 7, ssem.at[0], rsem1.at[i // GROUP], ahead(i))
        return c

    lax.fori_loop(1, n, send_pos, 0)

    def tiles_split(x):
        cat = jnp.concatenate(x, axis=1)
        for s, t in enumerate(split3(cat)):
            t = t.astype(BF)
            tst[s, 0:nt, :] = t
            tst[s, nt : 2 * nt, :] = t

    def send_edges(step):
        for u in range(2):
            a = pscr[pl.ds(s_halo[2 * u] * 8, 8), :]
            b = pscr[pl.ds(s_halo[2 * u + 1] * 8, 8), :]
            edge[pl.ds((2 * step + u) * 8, 8), :] = jnp.concatenate(
                [a[0:3], b[0:3], jnp.zeros((2, BLK), F32)], axis=0
            )
        pltpu.make_async_remote_copy(
            src_ref=edge.at[pl.ds(step * 16, 16), :],
            dst_ref=hrecv.at[pl.ds(step * 16, 16), :],
            send_sem=hssem.at[step],
            recv_sem=hsem.at[step],
            device_id=ahead(1),
            device_id_type=MESH,
        ).start()

    ready(3, 5)
    spread(s_pp, pscr, nt)
    pp = comps(pscr, nt)
    tiles_split(pp)
    send_edges(0)

    live = jnp.where(me > 0, 1.0, 0.0).astype(F32)
    sub_t = lax.broadcasted_iota(jnp.int32, (nt, BLK), 0)

    def halo_force(step):
        view = hrecv.at[pl.ds(step * 16, 16), :]
        pltpu.make_async_copy(view, view, hsem.at[step]).wait()
        out = [jnp.zeros((nt, BLK), F32) for _ in range(3)]
        for u in range(2):
            at = pl.ds((2 * step + u) * 8, 8)
            put_weights(ws, u, edge[at, :], hrecv[at, :])
            push = push_of(ws, u, edge[at, :], hrecv[at, :]) * live
            for k in range(2):
                here = sub_t == s_halo[2 * u + k]
                for c in range(3):
                    r = 3 * k + c
                    out[c] = out[c] + jnp.where(here, push[r : r + 1, :], 0.0)
        return out

    for k in range(2):
        sk_t[k] = jnp.transpose(sk_n[k].astype(F32)).astype(BF)
    ready(5, 9)
    bcopy.wait()

    def split_block(q, c):
        for s in range(2):
            b = jnp.transpose(bstage[2 * q + s])
            hi = b.astype(BF)
            bsplit[q, 0:BLK, s * BLK : (s + 1) * BLK] = hi
            bsplit[q, BLK : 2 * BLK, s * BLK : (s + 1) * BLK] = (
                b - hi.astype(F32)
            ).astype(BF)
        return c

    lax.fori_loop(0, nb // 2, split_block, 0, unroll=4)

    cmat = jnp.zeros((BLK, nb), F32)
    for m in range(NNZB):
        cmat = cmat + jnp.where(
            sub_b == s_pattern[m : m + 1, :], s_coup[m : m + 1, :], 0.0
        )
    cmat = jnp.transpose(pad_lanes(cmat))[0:nb]
    c_hi = cmat.astype(BF)
    c_lo = (cmat - c_hi.astype(F32)).astype(BF)
    vs[...] = jnp.zeros_like(vs)

    def matvec(x):
        for c in range(3):
            h, l = split2(x[c])
            vs[pl.ds(c, nb, stride=8), :] = h
            vs[pl.ds(3 + c, nb, stride=8), :] = l

        for q in range(nb // 2):
            at = pl.ds(q * 16, 16)
            t = vs[at, :].astype(BF)
            o = dot(jnp.concatenate([t, t], axis=1), bsplit[q])
            vo[at, :] = jnp.concatenate([o[0:8, :BLK], o[8:16, BLK:]], axis=0)
        a, b = comps(vo, nb), comps(vo, nb, 3)
        return [a[c] + b[c] for c in range(3)]

    def couple(v):
        h, l = split2(jnp.concatenate(v, axis=1))
        h, l = pad_rows(h.astype(BF)), pad_rows(l.astype(BF))
        o = dot(c_hi, h) + dot(c_lo, h) + dot(c_hi, l)
        return [o[:, c * BLK : (c + 1) * BLK] for c in range(3)]

    def solve(rhs):
        v = matvec(rhs)
        for _ in range(SWEEPS):
            w = couple(v)
            v = matvec([rhs[c] + w[c] for c in range(3)])
        return v

    def by_slot(ref, k):
        return jnp.concatenate(comps(ref, n, 3 * k), axis=1)

    def gather_sum(mats, ref):
        total = None
        for k in range(2):
            h, l = split2(by_slot(ref, k))
            o = dot(mats[k], h.astype(BF)) + dot(mats[k], l.astype(BF))
            total = o if total is None else total + o
        return [total[:, c * BLK : (c + 1) * BLK] for c in range(3)]

    def soil_sum(ref):
        return gather_sum([oh_t[0:nt, :], oh_t[nt : 2 * nt, :]], ref)

    def node_sum(ref):
        return gather_sum([sk_t[0, 0:nb, :], sk_t[1, 0:nb, :]], ref)

    lane_g = lax.broadcasted_iota(jnp.int32, (GROUP, BLK), 1)
    lane_gm = (lane_g & (nt - 1)).astype(F32)

    def pairs(g, near, far, push, react):
        for u in range(GROUP):
            at = tile_rows(g * GROUP + u)
            put_weights(ws, u, near[at, :], far[at, :])
        for u in range(GROUP):
            at = tile_rows(g * GROUP + u)
            react[at, :] = react_of(ws, u, near[at, :], far[at, :])
            push[at, :] = push_of(ws, u, near[at, :], far[at, :])

    def owner_group(g, c):
        base = pl.multiple_of(g * GROUP * 8, GROUP * 8)
        wait_rows(near1, rsem1.at[g], GROUP, 7)
        tid = near1[pl.ds(base + 6, GROUP, stride=8), :]
        oh = jnp.where(tid == lane_gm, 1.0, 0.0)
        sel = jnp.concatenate(
            [jnp.where(lane_g < nt, oh, 0.0), jnp.where(lane_g < nt, 0.0, oh)], axis=0
        ).astype(BF)
        got = dot(sel, tst[0]) + dot(sel, tst[1]) + dot(sel, tst[2])
        for k in range(2):
            for cc in range(3):
                far1[pl.ds(base + 3 * k + cc, GROUP, stride=8), :] = got[
                    k * GROUP : (k + 1) * GROUP, cc * BLK : (cc + 1) * BLK
                ]

        pairs(g, near1, far1, push1, react1)
        for u in range(GROUP):
            i = g * GROUP + u
            if u > 0:
                remote(push1, pret, i, 6, ssem.at[1], psem, behind(i))
            else:

                @pl.when(i > 0)
                def _():
                    remote(push1, pret, i, 6, ssem.at[1], psem, behind(i))

                @pl.when(i == 0)
                def _():
                    own(push1, pret, 6, psem)

        return c

    lax.fori_loop(0, n // GROUP, owner_group, 0)

    lane_m = (lane & (nt - 1)).astype(F32)
    oh_all = jnp.where(near1[pl.ds(6, n, stride=8), :] == lane_m, 1.0, 0.0)
    oh_n[0] = jnp.where(lane < nt, oh_all, 0.0).astype(BF)
    oh_n[1] = jnp.where(lane < nt, 0.0, oh_all).astype(BF)
    oh_t[...] = jnp.transpose(oh_all).astype(BF)

    hf = halo_force(0)
    sf = soil_sum(react1)
    spread(s_pv, pscr, nt)
    pv = comps(pscr, nt)
    pv = [pv[c] + time_step * (sf[c] + hf[c]) for c in range(3)]
    pp = [pp[c] + time_step * pv[c] for c in range(3)]
    put(pscr, nt, pp)
    tiles_split(pp)
    for k in range(2):
        got = dot(oh_n[k], tst[0]) + dot(oh_n[k], tst[1]) + dot(oh_n[k], tst[2])
        put(tsend, n, [got[:, c * BLK : (c + 1) * BLK] for c in range(3)], 3 * k)

    own(tsend, tret, 6, tsem.at[0])

    def send_tiles(i, c):
        remote(tsend, tret, i, 6, ssem.at[2], tsem.at[i // GROUP], behind(i))
        return c

    lax.fori_loop(1, n, send_tiles, 0)
    send_edges(1)

    spread(s_tv, nscr, nb)
    tv = comps(nscr, nb)
    wait_rows(pret, psem, n, 6)
    nf = node_sum(pret)
    tv = solve([tv[c] + time_step * nf[c] for c in range(3)])
    tp = [tp[c] + time_step * tv[c] for c in range(3)]
    node_slots(tp, near2)

    def node_group(g, c):
        wait_rows(tret, tsem.at[g], GROUP, 6)

        pairs(g, near2, tret, push2, react2)
        for u in range(GROUP):
            i = g * GROUP + u
            if u > 0:
                remote(react2, rret, i, 6, ssem.at[3], rrsem, ahead(i))
            else:

                @pl.when(i > 0)
                def _():
                    remote(react2, rret, i, 6, ssem.at[3], rrsem, ahead(i))

                @pl.when(i == 0)
                def _():
                    own(react2, rret, 6, rrsem)

        return c

    lax.fori_loop(0, n // GROUP, node_group, 0)

    nf = node_sum(push2)
    tv = solve([tv[c] + time_step * nf[c] for c in range(3)])
    tp = [tp[c] + time_step * tv[c] for c in range(3)]
    put(nscr, nb, tv)
    collect(nscr, o_tv, nb)
    put(nscr, nb, tp)
    collect(nscr, o_tp, nb)

    hf = halo_force(1)
    wait_rows(rret, rrsem, n, 6)
    sf = soil_sum(rret)
    pv = [pv[c] + time_step * (sf[c] + hf[c]) for c in range(3)]
    pp = [pp[c] + time_step * pv[c] for c in range(3)]
    put(pscr, nt, pv)
    collect(pscr, o_pv, nt)
    put(pscr, nt, pp)
    collect(pscr, o_pp, nt)

    wait_rows(send1, ssem.at[0], n - 1, 7)
    for s in range(1, 4):
        wait_rows(push1, ssem.at[s], n - 1, 6)
    for step in range(2):
        view = edge.at[pl.ds(step * 16, 16), :]
        pltpu.make_async_copy(view, view, hssem.at[step]).wait()


def hand_over(*refs):
    count = len(refs) // 2
    for k in range(count):
        refs[count + k][...] = refs[k][...]


def local(
    n,
    n_dom,
    tire_pos,
    tire_vel,
    part_pos,
    part_vel,
    contact_owner,
    contact_tile,
    halo_tiles,
    block_inverse,
    pattern,
    coupling,
):
    nb = tire_pos.shape[1] // BLK
    nt = part_pos.shape[1] // BLK
    vmem = pl.BlockSpec(memory_space=pltpu.VMEM)
    hbm = pl.BlockSpec(memory_space=pltpu.HBM)
    message = pltpu.VMEM((n * 8, BLK), F32)
    outs = (
        jax.ShapeDtypeStruct(tire_pos.shape, F32),
        jax.ShapeDtypeStruct(tire_pos.shape, F32),
        jax.ShapeDtypeStruct(part_pos.shape, F32),
        jax.ShapeDtypeStruct(part_pos.shape, F32),
    )
    results = pl.pallas_call(
        functools.partial(kernel, n, n_dom, nb, nt),
        out_shape=outs,
        in_specs=[hbm] * 10,
        out_specs=[vmem] * 4,
        scratch_shapes=[
            pltpu.VMEM(tire_pos.shape, F32),
            pltpu.VMEM(tire_pos.shape, F32),
            pltpu.VMEM(part_pos.shape, F32),
            pltpu.VMEM(part_pos.shape, F32),
            pltpu.VMEM((TOPC, nb), jnp.int32),
            pltpu.VMEM((TOPC, nb), jnp.int32),
            pltpu.SMEM((HB,), jnp.int32),
            pltpu.VMEM((NNZB, nb), jnp.int32),
            pltpu.VMEM((NNZB, nb), F32),
            pltpu.VMEM((GROUP, 2 * BLK, 2 * BLK), BF),
            pltpu.VMEM((nb, BLK, BLK), F32),
            pltpu.VMEM((nb // 2, 2 * BLK, 2 * BLK), BF),
            pltpu.VMEM((nb * 8, BLK), F32),
            pltpu.VMEM((nt * 8, BLK), F32),
        ]
        + [message] * 12
        + [
            pltpu.VMEM((32, BLK), F32),
            pltpu.VMEM((32, BLK), F32),
            pltpu.VMEM((16, BLK), F32),
            pltpu.VMEM((nb * 8, BLK), F32),
            pltpu.VMEM((nb * 8, BLK), F32),
            pltpu.VMEM((3, 2 * nt, 3 * BLK), BF),
            pltpu.VMEM((2, BLK, BLK), BF),
            pltpu.VMEM((2, BLK, BLK), BF),
            pltpu.VMEM((2, BLK, BLK), BF),
            pltpu.VMEM((BLK, BLK), BF),
            pltpu.SemaphoreType.DMA((9,)),
            pltpu.SemaphoreType.DMA,
            pltpu.SemaphoreType.DMA((4,)),
            pltpu.SemaphoreType.DMA((n // GROUP,)),
            pltpu.SemaphoreType.DMA,
            pltpu.SemaphoreType.DMA((n // GROUP,)),
            pltpu.SemaphoreType.DMA,
            pltpu.SemaphoreType.DMA((2,)),
            pltpu.SemaphoreType.DMA((2,)),
        ],
        compiler_params=pltpu.CompilerParams(
            collective_id=0, has_side_effects=True, vmem_limit_bytes=62 << 20
        ),
    )(
        tire_pos,
        tire_vel,
        part_pos,
        part_vel,
        contact_owner.T,
        contact_tile.T,
        halo_tiles,
        block_inverse,
        pattern.T,
        coupling.T,
    )
    return pl.pallas_call(
        hand_over,
        out_shape=outs,
        in_specs=[vmem] * 4,
        out_specs=[vmem] * 4,
        compiler_params=pltpu.CompilerParams(vmem_limit_bytes=62 << 20),
    )(*results)


def solution(mesh):
    n_role, n_dom = mesh.shape["role"], mesh.shape["dom"]
    both = ("role", "dom")
    return jax.shard_map(
        functools.partial(local, n_role * n_dom, n_dom),
        mesh=mesh,
        in_specs=(
            P(None, both),
            P(None, both),
            P(None, both),
            P(None, both),
            P(both, None),
            P(both, None),
            P(both),
            P(both, None, None),
            P(both, None),
            P(both, None),
        ),
        out_specs=(P(None, both), P(None, both), P(None, both), P(None, both)),
        check_vma=False,
    )
```
